512 devices in a mesh: dp: 64 (over z, x, core), tensor: 8 (over y).
Axes of the slice: x: 4, y: 8, z: 8, core: 2. Of those that a mesh axis runs over, the one named last changes fastest.
Arguments:
- hidden: bfloat16 [8192, 4096], P('dp', 'tensor'), may hold values from -6 to 6
- gain: bfloat16 [4096], P('tensor'), may hold values from 0.5 to 1.5
- w_query: bfloat16 [4096, 4096], P('dp', 'tensor'), may hold values from -0.09375 to 0.09375
- w_key: bfloat16 [4096, 1024], P('dp', 'tensor'), may hold values from -0.09375 to 0.09375
- w_value: bfloat16 [4096, 1024], P('dp', 'tensor'), may hold values from -0.09375 to 0.09375
- cotangent: bfloat16 [16384, 4096], P('dp', 'tensor'), may hold values from -6 to 6
- seq_length: int32 [64, 4], replicated, may hold values from 16 to 64, as said below
- home_offset: int32 [64, 4], replicated, may hold values from 0 to 112, as said below
- dest_shard: int32 [64, 4], replicated, may hold values from 0 to 63, as said below
- dest_offset: int32 [64, 4], replicated, may hold values from 0 to 192, as said below
Outputs:
- attention_output: bfloat16 [16384, 4096], P('dp', 'tensor')
- grad_hidden: bfloat16 [8192, 4096], P('dp', 'tensor')
- grad_value_weight: float32 [4096, 1024], P('dp', 'tensor')
The draws below stay inside these ranges and needn't reach their ends.
Inputs may be any that keep to these rules, and one draw needn't show every extreme that they name: `seq_length`: the 4 sequences of a shard fill its 128 rows exactly; every length is at least 16 and at most 64, and some sequence has length 64. `home_offset`: the sequences of a shard lie back to back from row 0 in the order of c. `dest_shard`: sequence c of shard h goes to shard (h + e) mod 64, e one of -1, 1, 32 and 33; every shard sends exactly one sequence to each of these 4 shards. `dest_offset`: the sequences that arrive at a shard lie back to back from row 0 of its 256 rows, in the order e = -1, 1, 32, 33; at some shard they fill all 256 rows.
All inputs are finite; a program needn't handle non-finite values.
Results may differ from the reference program's by a relative error of at most 0.02.
Values may be sent and summed in bfloat16 or wider, within the bound.
No kernel may reach another device: no remote copies, remote signals or barrier semaphores. Data moves between devices by JAX's collectives and lax.ppermute only.
A program may use at most 64 MiB of HBM per device.

```python
import jax
import jax.numpy as jnp
from jax import lax

D = 4096
HEADS = 32
KV_HEADS = 8
HEAD = 128
TOK_DEV = 128
SEQS = 4
CAP = 256
TOKENS = 8192
DEST_ROWS = 16384
N_DP = 64
N_TENSOR = 8


def shuffle_four(subkey):
    return jax.random.permutation(subkey, 4).astype(jnp.int32)


def plan_arrays(key):
    shard_count = N_DP
    shortest = TOK_DEV // 8
    stride_values = [-1, 1, N_DP // 2, N_DP // 2 + 1]
    subkeys = jax.random.split(key, 7)
    len_one = jax.random.randint(subkeys[0], (shard_count,), shortest, 3 * shortest + 1)
    len_two = jax.random.randint(subkeys[1], (shard_count,), shortest, 3 * shortest + 1)
    remainder = TOK_DEV - len_one - len_two
    len_three = jax.random.randint(subkeys[2], (shard_count,), jnp.maximum(shortest, remainder - 4 * shortest), jnp.minimum(4 * shortest, remainder - shortest) + 1)
    len_four = remainder - len_three
    lengths = jnp.stack([len_one, len_two, len_three, len_four], 1).astype(jnp.int32)
    center = jax.random.randint(subkeys[3], (), 0, shard_count)
    stride_array = jnp.array(stride_values, jnp.int32)
    forced_home = (center - stride_array + shard_count) % shard_count
    home_index = jnp.arange(shard_count, dtype=jnp.int32)
    hits = (home_index[:, None] == forced_home[None, :]).astype(jnp.int32)
    forced = jnp.sum(hits, 1) > 0
    forced_slot = jnp.sum(hits * jnp.arange(4, dtype=jnp.int32)[None, :], 1)
    part_one = jax.random.randint(subkeys[4], (shard_count,), shortest, 2 * shortest + 1)
    part_two = jax.random.randint(subkeys[5], (shard_count,), shortest, 3 * shortest - part_one + 1)
    part_three = 4 * shortest - part_one - part_two
    forced_lengths = jnp.stack([jnp.full((shard_count,), 4 * shortest, jnp.int32), part_one, part_two, part_three], 1).astype(jnp.int32)
    lengths = jnp.where(forced[:, None], forced_lengths, lengths)
    orders = jax.vmap(shuffle_four)(jax.random.split(subkeys[6], shard_count))
    column = jnp.arange(4, dtype=jnp.int32)[None, :]
    swapped = jnp.where(orders == forced_slot[:, None], orders[:, :1], jnp.where(column == 0, forced_slot[:, None], orders))
    orders = jnp.where(forced[:, None], swapped, orders).astype(jnp.int32)
    moves_of = stride_array[orders]
    targets = (home_index[:, None] + moves_of + shard_count) % shard_count
    by_slot = [jnp.sum(lengths * (orders == number), 1) for number in range(4)]
    incoming = jnp.stack([jnp.roll(by_slot[number], stride_values[number]) for number in range(4)], 1)
    starts = jnp.cumsum(incoming, 1) - incoming
    start_home = jnp.stack([jnp.roll(starts[:, number], -stride_values[number]) for number in range(4)], 1)
    dest_off = jnp.sum(jnp.stack([(orders == number) * start_home[:, number:number + 1] for number in range(4)], 0), 0)
    home_off = jnp.cumsum(lengths, 1) - lengths
    return (lengths.astype(jnp.int32), home_off.astype(jnp.int32), targets.astype(jnp.int32), dest_off.astype(jnp.int32))


def draw_seq_length(key, part):
    shared = plan_arrays(key)
    return shared[0]


def draw_home_offset(key, part):
    shared = plan_arrays(key)
    return shared[1]


def draw_dest_shard(key, part):
    shared = plan_arrays(key)
    return shared[2]


def draw_dest_offset(key, part):
    shared = plan_arrays(key)
    return shared[3]


def steps_of(own_key, dims, shards, smallest, largest):
    def one(dim, blocks):
        draws = jax.random.uniform(jax.random.fold_in(jax.random.fold_in(own_key, 6), dim), (blocks,), jnp.float32, smallest / len(shards), largest / len(shards))
        return jnp.repeat(jnp.exp(draws), dims[dim] // blocks).reshape((-1,) + (1,) * (len(dims) - dim - 1))

    loudness = one(*shards[0])
    for cut in shards[1:]:
        loudness = loudness * one(*cut)
    return loudness


def gaussian(stream_key, dims, spread, most, cuts=(), kind=jnp.bfloat16):
    entries = jax.random.normal(stream_key, dims, jnp.float32) * spread
    if len(cuts) > 0:
        entries = steps_of(stream_key, dims, cuts, -0.22, 0.18) * entries
    return jnp.clip(entries, min=-most, max=most).astype(kind)


def setup_inputs(seed: int = 0) -> dict:
    streams_of = jax.random.split(jax.random.key(seed), 11)
    hidden = gaussian(streams_of[0], (TOKENS, D), 1.0, 6.0, ((0, 64), (1, 8)))
    gain = jnp.clip(1.0 + 0.1 * jax.random.normal(streams_of[1], (D,), jnp.float32), 0.5, 1.5).astype(jnp.bfloat16)
    w_query = gaussian(streams_of[2], (D, HEADS * HEAD), D ** -0.5, 0.09375, ((0, 64), (1, 8)))
    w_key = gaussian(streams_of[3], (D, KV_HEADS * HEAD), D ** -0.5, 0.09375, ((0, 64), (1, 8)))
    w_value = gaussian(streams_of[4], (D, KV_HEADS * HEAD), D ** -0.5, 0.09375, ((0, 64), (1, 8)))
    cotangent = gaussian(streams_of[5], (DEST_ROWS, HEADS * HEAD), 1.0, 6.0, ((0, 64), (1, 8)))
    seq_length = draw_seq_length(jax.random.fold_in(streams_of[10], 71), 0)
    home_offset = draw_home_offset(jax.random.fold_in(streams_of[10], 71), 0)
    dest_shard = draw_dest_shard(jax.random.fold_in(streams_of[10], 71), 0)
    dest_offset = draw_dest_offset(jax.random.fold_in(streams_of[10], 71), 0)
    return {"hidden": hidden, "gain": gain, "w_query": w_query, "w_key": w_key, "w_value": w_value, "cotangent": cotangent, "seq_length": seq_length, "home_offset": home_offset, "dest_shard": dest_shard, "dest_offset": dest_offset}


EPSILON = 1e-05
ROPE_BASE = 500000.0

def rope_tables(position):
    half_head = HEAD // 2
    exponent = jnp.arange(half_head, dtype=jnp.float32) * (2.0 / HEAD)
    inverse = jnp.power(jnp.float32(ROPE_BASE), -exponent)
    angles = position.astype(jnp.float32)[:, None] * inverse[None, :]
    return (jnp.cos(angles)[:, None, :], jnp.sin(angles)[:, None, :])

def rotate(values, cosine, sine_part):
    half_head = values.shape[-1] // 2
    lower_half = values[..., :half_head]
    upper_half = values[..., half_head:]
    return jnp.concatenate([lower_half * cosine - upper_half * sine_part, upper_half * cosine + lower_half * sine_part], -1)

def unrotate(values, cosine, sine_part):
    half_head = values.shape[-1] // 2
    lower_half = values[..., :half_head]
    upper_half = values[..., half_head:]
    return jnp.concatenate([lower_half * cosine + upper_half * sine_part, upper_half * cosine - lower_half * sine_part], -1)

def attention_block(normed, w_query, w_key, w_value, cotangent, segment, position, occupied):
    row_count = normed.shape[0]
    kv_heads = w_key.shape[1] // HEAD
    q_heads = w_query.shape[1] // HEAD
    group_size = q_heads // kv_heads
    cosine, sine_part = rope_tables(position)
    query_rows = jnp.dot(normed, w_query, preferred_element_type=jnp.float32).reshape(row_count, q_heads, HEAD)
    key_rows = jnp.dot(normed, w_key, preferred_element_type=jnp.float32).reshape(row_count, kv_heads, HEAD)
    value_rows = jnp.dot(normed, w_value, preferred_element_type=jnp.float32).astype(jnp.bfloat16).reshape(row_count, kv_heads, HEAD)
    query_rows = rotate(query_rows, cosine, sine_part).astype(jnp.bfloat16).reshape(row_count, kv_heads, group_size, HEAD)
    key_rows = rotate(key_rows, cosine, sine_part).astype(jnp.bfloat16)
    factor = HEAD ** (-0.5)
    scores = jnp.einsum('qhgd,khd->hgqk', query_rows.astype(jnp.float32), key_rows.astype(jnp.float32)) * factor
    allowed = (segment[:, None] == segment[None, :]) & (position[None, :] <= position[:, None])
    scores = jnp.where(allowed[None, None], scores, jnp.float32(-1e+30))
    row_max = lax.optimization_barrier(jnp.max(scores, -1, keepdims=True))
    exp_terms = jnp.exp(scores - row_max)
    attn_prob = exp_terms / lax.optimization_barrier(jnp.sum(exp_terms, -1, keepdims=True))
    prob_low = attn_prob.astype(jnp.bfloat16)
    mixed_rows = jnp.einsum('hgqk,khd->qhgd', prob_low.astype(jnp.float32), value_rows.astype(jnp.float32))
    attn_out = jnp.where(occupied[:, None], mixed_rows.reshape(row_count, q_heads * HEAD), jnp.float32(0.0)).astype(jnp.bfloat16)
    grad_out = jnp.where(occupied[:, None], cotangent, jnp.zeros((), jnp.bfloat16)).reshape(row_count, kv_heads, group_size, HEAD)
    grad_value = jnp.einsum('hgqk,qhgd->khd', prob_low.astype(jnp.float32), grad_out.astype(jnp.float32)).astype(jnp.bfloat16)
    grad_probs = jnp.einsum('qhgd,khd->hgqk', grad_out.astype(jnp.float32), value_rows.astype(jnp.float32))
    centre = lax.optimization_barrier(jnp.sum(grad_probs * attn_prob, -1, keepdims=True))
    grad_scores = (attn_prob * (grad_probs - centre) * factor).astype(jnp.bfloat16)
    grad_query = jnp.einsum('hgqk,khd->qhgd', grad_scores.astype(jnp.float32), key_rows.astype(jnp.float32)).reshape(row_count, q_heads, HEAD)
    grad_key = jnp.einsum('hgqk,qhgd->khd', grad_scores.astype(jnp.float32), query_rows.astype(jnp.float32))
    grad_query = unrotate(grad_query, cosine, sine_part).astype(jnp.bfloat16).reshape(row_count, q_heads * HEAD)
    grad_key = unrotate(grad_key, cosine, sine_part).astype(jnp.bfloat16).reshape(row_count, kv_heads * HEAD)
    return (attn_out, grad_query, grad_key, grad_value.reshape(row_count, kv_heads * HEAD))

def group_product(grads, weights):
    return jnp.einsum('rpc,dpc->prd', grads.reshape(CAP, N_TENSOR, -1).astype(jnp.float32), weights.reshape(D, N_TENSOR, -1).astype(jnp.float32))

def reference(hidden, gain, w_query, w_key, w_value, cotangent, seq_length, home_offset, dest_shard, dest_offset):
    within = jnp.arange(TOK_DEV, dtype=jnp.int32)
    lower_bound = home_offset[:, None, :]
    upper_bound = (home_offset + seq_length)[:, None, :]
    member = ((within[None, :, None] >= lower_bound) & (within[None, :, None] < upper_bound)).astype(jnp.int32)
    start_home = lax.optimization_barrier(jnp.sum(member * lower_bound, -1))
    start_dest = lax.optimization_barrier(jnp.sum(member * (dest_shard * CAP + dest_offset)[:, None, :], -1))
    seq_index = jnp.arange(N_DP * SEQS, dtype=jnp.int32).reshape(N_DP, SEQS)
    seq_of_row = lax.optimization_barrier(jnp.sum(member * seq_index[:, None, :], -1)).reshape(-1)
    position_home = (within[None, :] - start_home).reshape(-1)
    target = (start_dest + within[None, :] - start_home).reshape(-1)
    dest_total = N_DP * CAP
    placed = jnp.zeros((dest_total, D), jnp.bfloat16).at[target].set(hidden)
    segment = jnp.full((dest_total,), -1, jnp.int32).at[target].set(seq_of_row)
    position = jnp.zeros((dest_total,), jnp.int32).at[target].set(position_home)
    gain_wide = gain.astype(jnp.float32)

    def one_shard(carry, shard):
        start = shard * CAP
        dest_rows = lax.dynamic_slice_in_dim(placed, start, CAP, 0)
        seg_rows = lax.dynamic_slice_in_dim(segment, start, CAP, 0)
        pos_rows = lax.dynamic_slice_in_dim(position, start, CAP, 0)
        cot_rows = lax.dynamic_slice_in_dim(cotangent, start, CAP, 0)
        occupied = seg_rows >= 0
        values = dest_rows.astype(jnp.float32)
        inverse_rms = lax.rsqrt(lax.optimization_barrier(jnp.mean(values * values, 1, keepdims=True)) + EPSILON)
        normed = (values * inverse_rms * gain_wide).astype(jnp.bfloat16)
        attn_out, grad_query, grad_key, grad_value = attention_block(normed, w_query, w_key, w_value, cot_rows, seg_rows, pos_rows, occupied)
        group_terms = group_product(grad_query, w_query) + group_product(grad_key, w_key) + group_product(grad_value, w_value)
        summed = lax.optimization_barrier(jnp.sum(lax.optimization_barrier(group_terms.astype(jnp.bfloat16)).astype(jnp.float32), 0))
        weighted = summed * gain_wide
        row_dot = lax.optimization_barrier(jnp.sum(weighted * values, 1, keepdims=True))
        grad_rows = (inverse_rms * weighted - values * inverse_rms ** 3 * row_dot / D).astype(jnp.bfloat16)
        grad_weight = carry + jnp.einsum('rd,rc->dc', normed.astype(jnp.float32), grad_value.astype(jnp.float32))
        return (grad_weight, (attn_out, grad_rows))
    grad_weight, (attn_all, grad_all) = lax.scan(one_shard, jnp.zeros((D, KV_HEADS * HEAD), jnp.float32), jnp.arange(N_DP, dtype=jnp.int32))
    attention_output = attn_all.reshape(dest_total, HEADS * HEAD)
    grad_hidden = grad_all.reshape(dest_total, D)[target]
    return (attention_output, grad_hidden, grad_weight)
```

```python
import functools

import jax
import jax.numpy as jnp
from jax import lax
from jax.experimental import pallas as pl
from jax.experimental.pallas import tpu as pltpu
from jax.sharding import PartitionSpec as P

D = 4096
HEAD = 128
TOK_DEV = 128
MAXLEN = 64
CAP = 256
SLOTS = 4
EXTRA = 16
EPSILON = 1e-05
ROPE_BASE = 500000.0
BF = jnp.bfloat16
F32 = jnp.float32
VMEM_BYTES = 48 * 1024 * 1024


def passed_along(value, axis, by):
    size = lax.axis_size(axis)
    return lax.ppermute(value, axis, [(i, (i + by) % size) for i in range(size)])


def picked(onehot, rows):
    return jnp.dot(onehot, rows, preferred_element_type=F32).astype(rows.dtype)


def dot_nn(a, b):
    return lax.dot_general(a, b, (((1,), (0,)), ((), ())), preferred_element_type=F32)


def dot_nt(a, b):
    return lax.dot_general(a, b, (((1,), (1,)), ((), ())), preferred_element_type=F32)


def dot_tn(a, b):
    return lax.dot_general(a, b, (((0,), (0,)), ((), ())), preferred_element_type=F32)


def layer_kernel(
    q_heads,
    rows_ref,
    w_ref,
    cot_ref,
    cos_ref,
    sin_ref,
    allowed_ref,
    cut_ref,
    attn_ref,
    terms_ref,
    value_terms_ref,
    inverse_ref,
    normed_ref,
    grads_ref,
):
    peers = rows_ref.shape[0]
    width = rows_ref.shape[2]
    kv_at = q_heads * HEAD
    squares = jnp.zeros((TOK_DEV, 1), F32)
    for j in range(peers):
        part = rows_ref[j, :TOK_DEV, :].astype(F32)
        squares = squares + jnp.sum(part * part, 1, keepdims=True)
    inverse = lax.rsqrt(squares / D + EPSILON)
    inverse_ref[...] = jnp.broadcast_to(inverse, inverse_ref.shape)
    projected = jnp.zeros((TOK_DEV, w_ref.shape[1]), F32)
    for j in range(peers):
        gain = rows_ref[j, TOK_DEV : TOK_DEV + EXTRA, :].astype(F32)[0:1, :]
        part = (rows_ref[j, :TOK_DEV, :].astype(F32) * inverse * gain).astype(BF)
        normed_ref[:, j * width : (j + 1) * width] = part
        projected = projected + dot_nn(part, w_ref[j * width : (j + 1) * width, :])
    cosine = cos_ref[...]
    sine = sin_ref[...]
    factor = HEAD ** (-0.5)
    allowed = allowed_ref[...] > 0.5
    key_raw = projected[:, kv_at : kv_at + HEAD]
    value_raw = projected[:, kv_at + HEAD :]
    key = (key_raw * cosine + pltpu.roll(key_raw, HEAD // 2, 1) * sine).astype(BF)
    value = value_raw.astype(BF)
    grad_key = jnp.zeros((TOK_DEV, HEAD), F32)
    grad_value = jnp.zeros((TOK_DEV, HEAD), F32)
    dots = jnp.zeros((TOK_DEV, HEAD), F32)
    cut = cut_ref[...]
    for g in range(q_heads):
        at = slice(g * HEAD, (g + 1) * HEAD)
        query_raw = projected[:, at]
        query = (query_raw * cosine + pltpu.roll(query_raw, HEAD // 2, 1) * sine).astype(BF)
        scores = jnp.where(allowed, dot_nt(query, key) * factor, F32(-1e30))
        exp_terms = jnp.exp(scores - jnp.max(scores, -1, keepdims=True))
        probs = exp_terms / jnp.sum(exp_terms, -1, keepdims=True)
        probs_low = probs.astype(BF)
        mixed = dot_nn(probs_low, value).astype(BF)
        attn_ref[:, at] = dot_nn(cut, mixed).astype(BF)
        grad_out = cot_ref[:, at]
        grad_value = grad_value + dot_tn(probs_low, grad_out)
        grad_probs = dot_nt(grad_out, value)
        centre = jnp.sum(grad_probs * probs, -1, keepdims=True)
        grad_scores = (probs * (grad_probs - centre) * factor).astype(BF)
        grad_query = dot_nn(grad_scores, key)
        grad_key = grad_key + dot_tn(grad_scores, query)
        grad_query = (grad_query * cosine - pltpu.roll(grad_query, HEAD // 2, 1) * sine).astype(BF)
        grads_ref[:, at] = grad_query
        dots = dots + grad_query.astype(F32) * query_raw
    grad_key = (grad_key * cosine - pltpu.roll(grad_key, HEAD // 2, 1) * sine).astype(BF)
    grad_value = grad_value.astype(BF)
    grads_ref[:, kv_at : kv_at + HEAD] = grad_key
    grads_ref[:, kv_at + HEAD :] = grad_value
    dots = dots + grad_key.astype(F32) * key_raw + grad_value.astype(F32) * value_raw
    share = jnp.sum(dots, 1, keepdims=True) / inverse
    share = jnp.transpose(jnp.broadcast_to(share, (TOK_DEV, TOK_DEV)))[0:EXTRA, :]
    high = share.astype(BF)
    low = (share - high.astype(F32)).astype(BF)
    blank = jnp.zeros((EXTRA, width - 2 * TOK_DEV), BF)
    tail = jnp.concatenate([high, low, blank], 1)
    grads = grads_ref[...]
    for j in range(peers):
        cols = slice(j * width, (j + 1) * width)
        value_terms_ref[cols, :] = dot_tn(normed_ref[:, cols], grad_value).astype(BF)
    for j in range(peers):
        cols = slice(j * width, (j + 1) * width)
        terms_ref[j, :TOK_DEV, :] = dot_nt(grads, w_ref[cols, :]).astype(BF)
        terms_ref[j, TOK_DEV:, :] = tail


def finish_kernel(terms_ref, hidden_ref, gain_ref, inverse_ref, out_ref):
    total = terms_ref[0].astype(F32)
    for j in range(1, terms_ref.shape[0]):
        total = total + terms_ref[j].astype(F32)
    share = total[TOK_DEV : TOK_DEV + 8, :]
    share = share[0:1, :TOK_DEV] + share[0:1, TOK_DEV : 2 * TOK_DEV]
    row_dot = jnp.transpose(jnp.broadcast_to(share, (TOK_DEV, TOK_DEV)))[:, 0:1]
    inverse = inverse_ref[:, 0:1]
    weighted = total[:TOK_DEV, :] * gain_ref[...].astype(F32)
    here = hidden_ref[...].astype(F32)
    out_ref[...] = (inverse * weighted - here * (inverse * inverse * inverse * row_dot / D)).astype(BF)


def in_vmem(count):
    return [pl.BlockSpec(memory_space=pltpu.VMEM)] * count


def on_device(
    hidden, gain, w_query, w_key, w_value, cotangent, seq_length, home_offset, dest_shard, dest_offset
):
    shards = lax.axis_size("dp")
    peers = lax.axis_size("tensor")
    me = lax.axis_index("dp")
    strides = [-1, 1, shards // 2, shards // 2 + 1]
    width = hidden.shape[1]
    q_cols = w_query.shape[1]
    k_cols = w_key.shape[1]
    q_heads = q_cols // HEAD

    weights = lax.all_gather(
        jnp.concatenate([w_query, w_key, w_value], 1), "dp", axis=0, tiled=True
    )
    packed = jnp.concatenate([hidden, jnp.broadcast_to(gain[None, :], (EXTRA, width))], 0)
    rows_full = lax.all_to_all(
        jnp.broadcast_to(packed[None], (peers, TOK_DEV + EXTRA, width)),
        "tensor", split_axis=0, concat_axis=0, tiled=True,
    )

    own_len = seq_length[me]
    own_off = home_offset[me]
    own_move = (dest_shard[me] - me + shards) % shards
    stride_mod = jnp.array([s % shards for s in strides], jnp.int32)
    chosen = (own_move[None, :] == stride_mod[:, None]).astype(jnp.int32)
    slot_len = jnp.sum(chosen * own_len[None, :], 1)
    slot_off = jnp.sum(chosen * own_off[None, :], 1)
    sources = (me - jnp.array(strides, jnp.int32) + shards) % shards
    source_move = (dest_shard[sources] - sources[:, None] + shards) % shards
    matches = (source_move == stride_mod[:, None]).astype(jnp.int32)
    in_len = jnp.sum(matches * seq_length[sources], 1)
    in_start = jnp.sum(matches * dest_offset[sources], 1)

    t = jnp.arange(MAXLEN, dtype=jnp.int32)
    dest_row = jnp.arange(CAP, dtype=jnp.int32)
    home_row = jnp.arange(TOK_DEV, dtype=jnp.int32)
    dest_onehot = (dest_row[None, None, :] == (in_start[:, None] + t[None, :])[:, :, None]) & (
        t[None, :, None] < in_len[:, None, None]
    )
    home_onehot = (home_row[None, None, :] == (slot_off[:, None] + t[None, :])[:, :, None]) & (
        t[None, :, None] < slot_len[:, None, None]
    )
    dest_onehot = dest_onehot.reshape(SLOTS * MAXLEN, CAP).astype(BF)
    home_onehot = home_onehot.reshape(SLOTS * MAXLEN, TOK_DEV).astype(BF)
    belongs = (home_row[None, :] >= slot_off[:, None]) & (
        home_row[None, :] < (slot_off + slot_len)[:, None]
    )
    segment = jnp.sum(belongs * jnp.arange(SLOTS, dtype=jnp.int32)[:, None], 0)
    position = jnp.sum(belongs * (home_row[None, :] - slot_off[:, None]), 0)
    allowed = (segment[:, None] == segment[None, :]) & (position[None, :] <= position[:, None])
    half = HEAD // 2
    exponent = jnp.arange(half, dtype=F32) * (2.0 / HEAD)
    angles = position.astype(F32)[:, None] * jnp.power(F32(ROPE_BASE), -exponent)[None, :]
    cosine, sine = jnp.cos(angles), jnp.sin(angles)
    cosine = jnp.concatenate([cosine, cosine], 1)
    sine = jnp.concatenate([-sine, sine], 1)

    cot_cut = picked(dest_onehot, cotangent).reshape(SLOTS, MAXLEN, q_cols)
    cot_back = jnp.concatenate(
        [passed_along(cot_cut[n], "dp", -s) for n, s in enumerate(strides)], 0
    )
    grad_out = picked(home_onehot.T, cot_back)

    attn_cut, terms, value_terms, inverse = pl.pallas_call(
        functools.partial(layer_kernel, q_heads),
        out_shape=(
            jax.ShapeDtypeStruct((SLOTS * MAXLEN, q_cols), BF),
            jax.ShapeDtypeStruct((peers, TOK_DEV + EXTRA, width), BF),
            jax.ShapeDtypeStruct((D, k_cols), BF),
            jax.ShapeDtypeStruct((TOK_DEV, HEAD), F32),
        ),
        in_specs=in_vmem(7),
        out_specs=tuple(in_vmem(4)),
        scratch_shapes=[
            pltpu.VMEM((TOK_DEV, D), BF),
            pltpu.VMEM((TOK_DEV, q_cols + 2 * k_cols), BF),
        ],
        compiler_params=pltpu.CompilerParams(vmem_limit_bytes=VMEM_BYTES),
        name="layer",
    )(rows_full, weights, grad_out, cosine, sine, allowed.astype(F32), home_onehot)

    rows_each = D // shards
    halves = value_terms.reshape(shards // 2, 2, rows_each, k_cols)
    core = me % 2
    kept = jnp.where(core == 0, halves[:, 0], halves[:, 1])
    given = jnp.where(core == 0, halves[:, 1], halves[:, 0])
    got = lax.ppermute(given, "dp", [(i, i ^ 1) for i in range(shards)])
    pair = (kept.astype(F32) + got.astype(F32)).astype(BF)
    parts = lax.all_to_all(
        pair, "dp", split_axis=0, concat_axis=0, tiled=True,
        axis_index_groups=[list(range(c, shards, 2)) for c in range(2)],
    )
    grad_value_weight = jnp.sum(parts.astype(F32), 0)

    summed = lax.all_to_all(terms, "tensor", split_axis=0, concat_axis=0, tiled=True)
    grad_hidden = pl.pallas_call(
        finish_kernel,
        out_shape=jax.ShapeDtypeStruct((TOK_DEV, width), BF),
        in_specs=in_vmem(4),
        out_specs=in_vmem(1)[0],
        compiler_params=pltpu.CompilerParams(vmem_limit_bytes=VMEM_BYTES),
        name="finish",
    )(summed, hidden, gain[None, :], inverse)

    attn_cut = attn_cut.reshape(SLOTS, MAXLEN, q_cols)
    attn_sent = jnp.concatenate(
        [passed_along(attn_cut[n], "dp", s) for n, s in enumerate(strides)], 0
    )
    attn_out = picked(dest_onehot.T, attn_sent)
    return (attn_out, grad_hidden, grad_value_weight)


def solution(mesh):
    return jax.shard_map(
        on_device,
        mesh=mesh,
        in_specs=(P("dp", "tensor"), P("tensor")) + (P("dp", "tensor"),) * 4 + (P(),) * 4,
        out_specs=(P("dp", "tensor"), P("dp", "tensor"), P("dp", "tensor")),
        check_vma=False,
    )
```

```python
import functools

import jax
import jax.numpy as jnp
import numpy as np
from jax import lax
from jax.experimental import pallas as pl
from jax.experimental.pallas import tpu as pltpu
from jax.sharding import PartitionSpec as P

D = 4096
HEAD = 128
TOK_DEV = 128
MAXLEN = 64
CAP = 256
SLOTS = 4
EXTRA = 16
EPSILON = 1e-05
ROPE_BASE = 500000.0
NZ, NX, NC = 8, 4, 2
BF = jnp.bfloat16
F32 = jnp.float32
VMEM_BYTES = 48 * 1024 * 1024


def moved(value, where):
    pairs = []
    for z in range(NZ):
        for x in range(NX):
            for c in range(NC):
                tz, tx, tc = where(z, x, c)
                pairs.append(((z * NX + x) * NC + c, ((tz % NZ) * NX + tx % NX) * NC + tc))
    return lax.ppermute(value, "dp", pairs)


def other_core(value):
    return moved(value, lambda z, x, c: (z, x, 1 - c))


def along_z(value):
    return moved(value, lambda z, x, c: (z + (1 if c == 0 else -1), x, c))


def passed_along(value, by):
    size = lax.axis_size("dp")
    return lax.ppermute(value, "dp", [(i, (i + by) % size) for i in range(size)])


def dot_nn(a, b):
    return lax.dot_general(a, b, (((1,), (0,)), ((), ())), preferred_element_type=F32)


def dot_nt(a, b):
    return lax.dot_general(a, b, (((1,), (1,)), ((), ())), preferred_element_type=F32)


def dot_tn(a, b):
    return lax.dot_general(a, b, (((0,), (0,)), ((), ())), preferred_element_type=F32)


def place():
    me = lax.axis_index("dp")
    return me, me // (NX * NC), (me // NC) % NX, me % NC


def plan_kernel(
    strides, shards,
    len_ref, off_ref, shard_ref, start_ref, freq_ref, cotangent_ref,
    cut0_ref, cut1_ref, cut2_ref, cut3_ref, home_ref, dest_ref, cos_ref, sin_ref, allowed_ref,
):
    me = lax.axis_index("dp")
    rows = lax.broadcasted_iota(jnp.int32, (TOK_DEV, TOK_DEV), 0)
    cols = lax.broadcasted_iota(jnp.int32, (TOK_DEV, TOK_DEV), 1)
    row_seq, row_pos = jnp.zeros_like(rows), jnp.zeros_like(rows)
    col_seq, col_pos = jnp.zeros_like(rows), jnp.zeros_like(rows)
    cuts = (cut0_ref, cut1_ref, cut2_ref, cut3_ref)
    for e, stride in enumerate(strides):
        target = lax.rem(me + stride + shards, shards)
        source = lax.rem(me - stride + shards, shards)
        length = jnp.int32(0)
        offset = jnp.int32(0)
        in_len = jnp.int32(0)
        in_start = jnp.int32(0)
        for c in range(SLOTS):
            mine = shard_ref[c, me] == target
            length = length + jnp.where(mine, len_ref[c, me], 0)
            offset = offset + jnp.where(mine, off_ref[c, me], 0)
            theirs = shard_ref[c, source] == me
            in_len = in_len + jnp.where(theirs, len_ref[c, source], 0)
            in_start = in_start + jnp.where(theirs, start_ref[c, source], 0)
        inside = (rows >= offset) & (rows < offset + length)
        row_seq = jnp.where(inside, e, row_seq)
        row_pos = jnp.where(inside, rows - offset, row_pos)
        inside = (cols >= offset) & (cols < offset + length)
        col_seq = jnp.where(inside, e, col_seq)
        col_pos = jnp.where(inside, cols - offset, col_pos)
        at = slice(e * MAXLEN, (e + 1) * MAXLEN)
        t = lax.broadcasted_iota(jnp.int32, (MAXLEN, TOK_DEV), 0)
        r = lax.broadcasted_iota(jnp.int32, (MAXLEN, TOK_DEV), 1)
        home_ref[at, :] = jnp.where((r == t + offset) & (t < length), 1.0, 0.0).astype(BF)
        t = lax.broadcasted_iota(jnp.int32, (MAXLEN, CAP), 0)
        r = lax.broadcasted_iota(jnp.int32, (MAXLEN, CAP), 1)
        dest = jnp.where((r == t + in_start) & (t < in_len), 1.0, 0.0).astype(BF)
        dest_ref[at, :] = dest
        cuts[e][...] = dot_nn(dest, cotangent_ref[...]).astype(BF)
    allowed_ref[...] = jnp.where((row_seq == col_seq) & (col_pos <= row_pos), 1.0, 0.0)
    angles = row_pos.astype(F32) * freq_ref[...]
    cos_ref[...] = jnp.cos(angles)
    sine = jnp.sin(angles)
    sin_ref[...] = jnp.where(cols < HEAD // 2, -sine, sine)


def layer_kernel(q_heads, pieces, *refs):
    rows_ref, cos_ref, sin_ref, allowed_ref, home_ref = refs[:5]
    cot_refs = refs[5:9]
    w_refs = refs[9 : 9 + pieces]
    cut0_ref, cut1_ref, cut2_ref, cut3_ref, terms_ref, kept_ref, given_ref, inverse_ref = refs[9 + pieces : 17 + pieces]
    normed_ref, grads_ref = refs[17 + pieces :]
    _, z, x, c = place()
    up = 1 - 2 * c
    where = [(z, 0, w_refs[0], 0), (z, 1, w_refs[0], 256)]
    for k in range(1, NZ // 2):
        first = 1 + 4 * (k - 1)
        behind = lax.rem(z - up * k + NZ, NZ)
        ahead = lax.rem(z + up * k + NZ, NZ)
        where.append((behind, c, w_refs[first], 0))
        where.append((behind, 1 - c, w_refs[first + 1], 0))
        where.append((ahead, 1 - c, w_refs[first + 2], 0))
        where.append((ahead, c, w_refs[first + 3], 0))
    far = lax.rem(z + NZ // 2, NZ)
    where.append((far, c, w_refs[pieces - 2], 0))
    where.append((far, 1 - c, w_refs[pieces - 1], 0))
    deep = rows_ref.shape[3]
    kv_at = q_heads * HEAD
    squares = jnp.zeros((TOK_DEV, 1), F32)
    for j in range(NZ):
        for h in range(2):
            part = rows_ref[j, h, :TOK_DEV, :].astype(F32)
            squares = squares + jnp.sum(part * part, 1, keepdims=True)
    inverse = lax.rsqrt(squares / D + EPSILON)
    inverse_ref[...] = jnp.broadcast_to(inverse, inverse_ref.shape)
    projected = jnp.zeros((TOK_DEV, w_refs[0].shape[1]), F32)
    for n, (block, half, w_ref, at) in enumerate(where):
        gain = rows_ref[block, half, TOK_DEV:, :].astype(F32)[0:1, :]
        part = (rows_ref[block, half, :TOK_DEV, :].astype(F32) * inverse * gain).astype(BF)
        normed_ref[n] = part
        projected = projected + dot_nn(part, w_ref[at : at + deep, :])
    cosine = cos_ref[...]
    sine = sin_ref[...]
    factor = HEAD ** (-0.5)
    allowed = allowed_ref[...] > 0.5
    home = home_ref[...]
    cot = jnp.concatenate([ref[...] for ref in cot_refs], 0)
    cot = dot_tn(home, cot).astype(BF)
    key_raw = projected[:, kv_at : kv_at + HEAD]
    value_raw = projected[:, kv_at + HEAD :]
    key = (key_raw * cosine + pltpu.roll(key_raw, HEAD // 2, 1) * sine).astype(BF)
    value = value_raw.astype(BF)
    grad_key = jnp.zeros((TOK_DEV, HEAD), F32)
    grad_value = jnp.zeros((TOK_DEV, HEAD), F32)
    dots = jnp.zeros((TOK_DEV, HEAD), F32)
    cuts = (cut0_ref, cut1_ref, cut2_ref, cut3_ref)
    for g in range(q_heads):
        at = slice(g * HEAD, (g + 1) * HEAD)
        query_raw = projected[:, at]
        query = (query_raw * cosine + pltpu.roll(query_raw, HEAD // 2, 1) * sine).astype(BF)
        scores = jnp.where(allowed, dot_nt(query, key) * factor, F32(-1e30))
        exp_terms = jnp.exp(scores - jnp.max(scores, -1, keepdims=True))
        probs = exp_terms / jnp.sum(exp_terms, -1, keepdims=True)
        probs_low = probs.astype(BF)
        mixed = dot_nn(probs_low, value).astype(BF)
        mixed = dot_nn(home, mixed).astype(BF)
        for e in range(SLOTS):
            cuts[e][:, at] = mixed[e * MAXLEN : (e + 1) * MAXLEN, :]
        grad_out = cot[:, at]
        grad_value = grad_value + dot_tn(probs_low, grad_out)
        grad_probs = dot_nt(grad_out, value)
        centre = jnp.sum(grad_probs * probs, -1, keepdims=True)
        grad_scores = (probs * (grad_probs - centre) * factor).astype(BF)
        grad_query = dot_nn(grad_scores, key)
        grad_key = grad_key + dot_tn(grad_scores, query)
        grad_query = (grad_query * cosine - pltpu.roll(grad_query, HEAD // 2, 1) * sine).astype(BF)
        grads_ref[:, at] = grad_query
        dots = dots + grad_query.astype(F32) * query_raw
    grad_key = (grad_key * cosine - pltpu.roll(grad_key, HEAD // 2, 1) * sine).astype(BF)
    grad_value = grad_value.astype(BF)
    grads_ref[:, kv_at : kv_at + HEAD] = grad_key
    grads_ref[:, kv_at + HEAD :] = grad_value
    dots = dots + grad_key.astype(F32) * key_raw + grad_value.astype(F32) * value_raw
    share = jnp.sum(dots, 1, keepdims=True) / inverse
    share = jnp.transpose(jnp.broadcast_to(share, (TOK_DEV, TOK_DEV)))[0:EXTRA, :]
    high = share.astype(BF)
    low = (share - high.astype(F32)).astype(BF)
    tail = jnp.concatenate([high, low], 1)
    grads = grads_ref[...]
    for n, (block, half, w_ref, at) in enumerate(where):
        found = dot_tn(normed_ref[n], grad_value).astype(BF)
        for pair in range(2):
            low_rows = found[pair * 128 : pair * 128 + 64, :]
            high_rows = found[pair * 128 + 64 : (pair + 1) * 128, :]
            away = lax.rem(2 * half + pair - x + NX, NX)
            kept_ref[away, block] = jnp.where(c == 0, low_rows, high_rows)
            given_ref[away, block] = jnp.where(c == 0, high_rows, low_rows)
    for n, (block, half, w_ref, at) in enumerate(where):
        terms_ref[block, half, :TOK_DEV, :] = dot_nt(grads, w_ref[at : at + deep, :]).astype(BF)
        terms_ref[block, half, TOK_DEV:, :] = tail


def finish_kernel(terms_ref, hidden_ref, gain_ref, inverse_ref, out_ref):
    inverse = inverse_ref[:, 0:1]
    deep = terms_ref.shape[3]
    row_dot = None
    for h in range(2):
        total = terms_ref[0, h].astype(F32)
        for j in range(1, terms_ref.shape[0]):
            total = total + terms_ref[j, h].astype(F32)
        if row_dot is None:
            share = total[TOK_DEV : TOK_DEV + 8, :]
            share = share[0:1, :TOK_DEV] + share[0:1, TOK_DEV : 2 * TOK_DEV]
            row_dot = jnp.transpose(jnp.broadcast_to(share, (TOK_DEV, TOK_DEV)))[:, 0:1]
        at = slice(h * deep, (h + 1) * deep)
        weighted = total[:TOK_DEV, :] * gain_ref[:, at].astype(F32)
        here = hidden_ref[:, at].astype(F32)
        out_ref[:, at] = (inverse * weighted - here * (inverse * inverse * inverse * row_dot / D)).astype(BF)


def lay_kernel(dest_ref, a_ref, b_ref, c_ref, d_ref, out_ref):
    rows = jnp.concatenate([a_ref[...], b_ref[...], c_ref[...], d_ref[...]], 0)
    out_ref[...] = dot_tn(dest_ref[...], rows).astype(BF)


def in_vmem(count):
    return [pl.BlockSpec(memory_space=pltpu.VMEM)] * count


def kernel_call(body, outs, ins, name, scratch=()):
    shapes = [jax.ShapeDtypeStruct(s, d) for s, d in outs]
    return pl.pallas_call(
        body,
        out_shape=shapes,
        in_specs=ins,
        out_specs=in_vmem(len(shapes)),
        scratch_shapes=list(scratch),
        compiler_params=pltpu.CompilerParams(vmem_limit_bytes=VMEM_BYTES),
        name=name,
    )


def on_device(
    hidden, gain, w_query, w_key, w_value, cotangent, seq_length, home_offset, dest_shard, dest_offset
):
    shards = lax.axis_size("dp")
    peers = lax.axis_size("tensor")
    me, z, x, c = place()
    strides = [-1, 1, shards // 2, shards // 2 + 1]
    width = hidden.shape[1]
    deep = width // 2
    q_cols = w_query.shape[1]
    k_cols = w_key.shape[1]
    q_heads = q_cols // HEAD
    rows_each = D // shards

    own = jnp.concatenate([w_query, w_key, w_value], 1)
    slab = lax.all_gather(
        own, "dp", axis=0, tiled=True,
        axis_index_groups=[[a * NX * NC + b for b in range(NX * NC)] for a in range(NZ)],
    )
    first = jnp.where(c == 0, slab[:deep], slab[deep:])
    second = jnp.where(c == 0, slab[deep:], slab[:deep])
    weights = [slab]
    for _ in range(1, NZ // 2):
        first, second = along_z(first), along_z(second)
        weights += [first, second, other_core(first), other_core(second)]
    first = along_z(first)
    weights += [first, other_core(first)]

    packed = jnp.concatenate([hidden, jnp.broadcast_to(gain[None, :], (EXTRA, width))], 0)
    packed = packed.reshape(TOK_DEV + EXTRA, 2, deep).transpose(1, 0, 2)
    rows_full = lax.all_to_all(
        jnp.broadcast_to(packed[None], (peers,) + packed.shape),
        "tensor", split_axis=0, concat_axis=0, tiled=True,
    )

    half = HEAD // 2
    freq = np.power(np.float32(ROPE_BASE), -(np.arange(half, dtype=np.float32) * np.float32(2.0 / HEAD)))
    freq = jnp.asarray(np.concatenate([freq, freq])[None, :].astype(np.float32))
    smem = [pl.BlockSpec(memory_space=pltpu.SMEM)] * 4
    square = ((TOK_DEV, TOK_DEV), F32)
    cut = ((MAXLEN, q_cols), BF)
    *cot_cuts, home, dest, cosine, sine, allowed = kernel_call(
        functools.partial(plan_kernel, strides, shards),
        [cut] * 4 + [((SLOTS * MAXLEN, TOK_DEV), BF), ((SLOTS * MAXLEN, CAP), BF)] + [square] * 3,
        smem + in_vmem(2),
        "plan",
    )(seq_length.T, home_offset.T, dest_shard.T, dest_offset.T, freq, cotangent)
    cots = [passed_along(cot_cuts[n], -s) for n, s in enumerate(strides)]

    pieces = len(weights)
    share = ((NX, NZ, rows_each, k_cols), BF)
    *attn_cuts, terms, kept, given, inverse = kernel_call(
        functools.partial(layer_kernel, q_heads, pieces),
        [cut] * 4 + [((peers, 2, TOK_DEV + EXTRA, deep), BF), share, share, square],
        in_vmem(9 + pieces),
        "layer",
        [
            pltpu.VMEM((2 * NZ, TOK_DEV, deep), BF),
            pltpu.VMEM((TOK_DEV, q_cols + 2 * k_cols), BF),
        ],
    )(rows_full, cosine, sine, allowed, home, *cots, *weights)

    summed = lax.all_to_all(terms, "tensor", split_axis=0, concat_axis=0, tiled=True)
    (grad_hidden,) = kernel_call(
        finish_kernel, [((TOK_DEV, width), BF)], in_vmem(4), "finish"
    )(summed, hidden, gain[None, :], inverse)

    attn_sent = [passed_along(attn_cuts[n], s) for n, s in enumerate(strides)]
    (attn_out,) = kernel_call(lay_kernel, [((CAP, q_cols), BF)], in_vmem(5), "lay")(dest, *attn_sent)

    pair = kept.astype(F32) + other_core(given).astype(F32)
    total = pair[0]
    for k in range(1, NX):
        total = total + moved(pair[k].astype(BF), lambda z, x, c, k=k: (z, x + k, c)).astype(F32)
    span = NZ // 2
    while span:
        upper = (z // span) % 2
        mine = jnp.where(upper == 0, total[:span], total[span:])
        theirs = jnp.where(upper == 0, total[span:], total[:span])
        if span > 1:
            theirs = theirs.astype(BF)
        total = mine + moved(theirs, lambda z, x, c, s=span: (z ^ s, x, c)).astype(F32)
        span //= 2
    grad_value_weight = total.reshape(rows_each, k_cols)
    return (attn_out, grad_hidden, grad_value_weight)


def solution(mesh):
    return jax.shard_map(
        on_device,
        mesh=mesh,
        in_specs=(P("dp", "tensor"), P("tensor")) + (P("dp", "tensor"),) * 4 + (P(),) * 4,
        out_specs=(P("dp", "tensor"), P("dp", "tensor"), P("dp", "tensor")),
        check_vma=False,
    )
```

```python
import functools

import jax
import jax.numpy as jnp
import numpy as np
from jax import lax
from jax.experimental import pallas as pl
from jax.experimental.pallas import tpu as pltpu
from jax.sharding import PartitionSpec as P

D = 4096
HEAD = 128
TOK_DEV = 128
MAXLEN = 64
CAP = 256
SLOTS = 4
EXTRA = 16
EPSILON = 1e-05
ROPE_BASE = 500000.0
NZ, NX, NC = 8, 4, 2
BF = jnp.bfloat16
F32 = jnp.float32
MIB = 1024 * 1024


def moved(value, where):
    pairs = []
    for z in range(NZ):
        for x in range(NX):
            for c in range(NC):
                tz, tx, tc = where(z, x, c)
                pairs.append(((z * NX + x) * NC + c, ((tz % NZ) * NX + tx % NX) * NC + tc))
    return lax.ppermute(value, "dp", pairs)


def other_core(value):
    return moved(value, lambda z, x, c: (z, x, 1 - c))


def along_z(value):
    return moved(value, lambda z, x, c: (z + (1 if c == 0 else -1), x, c))


def passed_along(value, by):
    size = lax.axis_size("dp")
    return lax.ppermute(value, "dp", [(i, (i + by) % size) for i in range(size)])


def tied(*values):
    return lax.optimization_barrier(values)


def dot_nn(a, b):
    return lax.dot_general(a, b, (((1,), (0,)), ((), ())), preferred_element_type=F32)


def dot_nt(a, b):
    return lax.dot_general(a, b, (((1,), (1,)), ((), ())), preferred_element_type=F32)


def dot_tn(a, b):
    return lax.dot_general(a, b, (((0,), (0,)), ((), ())), preferred_element_type=F32)


def place():
    me = lax.axis_index("dp")
    return me, me // (NX * NC), (me // NC) % NX, me % NC


def plan_kernel(
    strides, shards, get, put, send, smem, extra,
):
    len_ref, off_ref, shard_ref, start_ref = smem
    home_ref, dest_ref, cos_ref, sin_ref, allowed_ref = [put(SLOTS + i) for i in range(5)]
    me = lax.axis_index("dp")
    rows = lax.broadcasted_iota(jnp.int32, (TOK_DEV, TOK_DEV), 0)
    cols = lax.broadcasted_iota(jnp.int32, (TOK_DEV, TOK_DEV), 1)
    row_seq, row_pos = jnp.zeros_like(rows), jnp.zeros_like(rows)
    col_seq, col_pos = jnp.zeros_like(rows), jnp.zeros_like(rows)
    for e, stride in enumerate(strides):
        target = lax.rem(me + stride + shards, shards)
        source = lax.rem(me - stride + shards, shards)
        length = jnp.int32(0)
        offset = jnp.int32(0)
        in_len = jnp.int32(0)
        in_start = jnp.int32(0)
        for c in range(SLOTS):
            mine = shard_ref[c, me] == target
            length = length + jnp.where(mine, len_ref[c, me], 0)
            offset = offset + jnp.where(mine, off_ref[c, me], 0)
            theirs = shard_ref[c, source] == me
            in_len = in_len + jnp.where(theirs, len_ref[c, source], 0)
            in_start = in_start + jnp.where(theirs, start_ref[c, source], 0)
        inside = (rows >= offset) & (rows < offset + length)
        row_seq = jnp.where(inside, e, row_seq)
        row_pos = jnp.where(inside, rows - offset, row_pos)
        inside = (cols >= offset) & (cols < offset + length)
        col_seq = jnp.where(inside, e, col_seq)
        col_pos = jnp.where(inside, cols - offset, col_pos)
        at = slice(e * MAXLEN, (e + 1) * MAXLEN)
        t = lax.broadcasted_iota(jnp.int32, (MAXLEN, TOK_DEV), 0)
        r = lax.broadcasted_iota(jnp.int32, (MAXLEN, TOK_DEV), 1)
        home_ref[at, :] = jnp.where((r == t + offset) & (t < length), 1.0, 0.0).astype(BF)
        t = lax.broadcasted_iota(jnp.int32, (MAXLEN, CAP), 0)
        r = lax.broadcasted_iota(jnp.int32, (MAXLEN, CAP), 1)
        dest = jnp.where((r == t + in_start) & (t < in_len), 1.0, 0.0).astype(BF)
        dest_ref[at, :] = dest
        put(e)[...] = dot_nn(dest, get(1)[...]).astype(BF)
        send(e)
    allowed_ref[...] = jnp.where((row_seq == col_seq) & (col_pos <= row_pos), 1.0, 0.0)
    angles = row_pos.astype(F32) * get(0)[...]
    cos_ref[...] = jnp.cos(angles)
    sine = jnp.sin(angles)
    sin_ref[...] = jnp.where(cols < HEAD // 2, -sine, sine)


def layer_kernel(q_heads, pieces, peers, get, put, send, smem, extra):
    normed_ref, grads_ref, terms_ref = extra
    kept_ref, given_ref, inverse_ref = [put(SLOTS + i) for i in range(3)]
    out_at = SLOTS + 3
    peer = lax.axis_index("tensor")
    w_refs = list(range(9, 9 + pieces))
    _, z, x, c = place()
    up = 1 - 2 * c
    where = [(z, 0, w_refs[0], 0), (z, 1, w_refs[0], 256)]
    for k in range(1, NZ // 2):
        first = 1 + 4 * (k - 1)
        behind = lax.rem(z - up * k + NZ, NZ)
        ahead = lax.rem(z + up * k + NZ, NZ)
        where.append((behind, c, w_refs[first], 0))
        where.append((behind, 1 - c, w_refs[first + 1], 0))
        where.append((ahead, 1 - c, w_refs[first + 2], 0))
        where.append((ahead, c, w_refs[first + 3], 0))
    far = lax.rem(z + NZ // 2, NZ)
    where.append((far, c, w_refs[pieces - 2], 0))
    where.append((far, 1 - c, w_refs[pieces - 1], 0))
    rows_ref = get(0)
    deep = rows_ref.shape[3]
    kv_at = q_heads * HEAD
    squares = jnp.zeros((TOK_DEV, 1), F32)
    for j in range(NZ):
        for h in range(2):
            part = rows_ref[j, h, :TOK_DEV, :].astype(F32)
            squares = squares + jnp.sum(part * part, 1, keepdims=True)
    inverse = lax.rsqrt(squares / D + EPSILON)
    inverse_ref[...] = jnp.broadcast_to(inverse, inverse_ref.shape)
    projected = jnp.zeros((TOK_DEV, kv_at + 2 * HEAD), F32)
    for n, (block, half, w_ref, at) in enumerate(where):
        gain = rows_ref[block, half, TOK_DEV:, :].astype(F32)[0:1, :]
        part = (rows_ref[block, half, :TOK_DEV, :].astype(F32) * inverse * gain).astype(BF)
        normed_ref[n] = part
        projected = projected + dot_nn(part, get(w_ref)[at : at + deep, :])
    cosine = get(1)[...]
    sine = get(2)[...]
    factor = HEAD ** (-0.5)
    allowed = get(3)[...] > 0.5
    home = get(4)[...]
    cot = jnp.concatenate([get(5 + e)[...] for e in range(SLOTS)], 0)
    cot = dot_tn(home, cot).astype(BF)
    key_raw = projected[:, kv_at : kv_at + HEAD]
    value_raw = projected[:, kv_at + HEAD :]
    key = (key_raw * cosine + pltpu.roll(key_raw, HEAD // 2, 1) * sine).astype(BF)
    value = value_raw.astype(BF)
    grad_key = jnp.zeros((TOK_DEV, HEAD), F32)
    grad_value = jnp.zeros((TOK_DEV, HEAD), F32)
    dots = jnp.zeros((TOK_DEV, HEAD), F32)
    for g in range(q_heads):
        at = slice(g * HEAD, (g + 1) * HEAD)
        query_raw = projected[:, at]
        query = (query_raw * cosine + pltpu.roll(query_raw, HEAD // 2, 1) * sine).astype(BF)
        scores = jnp.where(allowed, dot_nt(query, key) * factor, F32(-1e30))
        exp_terms = jnp.exp(scores - jnp.max(scores, -1, keepdims=True))
        probs = exp_terms / jnp.sum(exp_terms, -1, keepdims=True)
        probs_low = probs.astype(BF)
        mixed = dot_nn(probs_low, value).astype(BF)
        mixed = dot_nn(home, mixed).astype(BF)
        for e in range(SLOTS):
            put(e)[:, at] = mixed[e * MAXLEN : (e + 1) * MAXLEN, :]
        grad_out = cot[:, at]
        grad_value = grad_value + dot_tn(probs_low, grad_out)
        grad_probs = dot_nt(grad_out, value)
        centre = jnp.sum(grad_probs * probs, -1, keepdims=True)
        grad_scores = (probs * (grad_probs - centre) * factor).astype(BF)
        grad_query = dot_nn(grad_scores, key)
        grad_key = grad_key + dot_tn(grad_scores, query)
        grad_query = (grad_query * cosine - pltpu.roll(grad_query, HEAD // 2, 1) * sine).astype(BF)
        grads_ref[:, at] = grad_query
        dots = dots + grad_query.astype(F32) * query_raw
    grad_key = (grad_key * cosine - pltpu.roll(grad_key, HEAD // 2, 1) * sine).astype(BF)
    grad_value = grad_value.astype(BF)
    grads_ref[:, kv_at : kv_at + HEAD] = grad_key
    grads_ref[:, kv_at + HEAD :] = grad_value
    dots = dots + grad_key.astype(F32) * key_raw + grad_value.astype(F32) * value_raw
    for e in range(SLOTS):
        send(e)
    share = jnp.sum(dots, 1, keepdims=True) / inverse
    share = jnp.transpose(jnp.broadcast_to(share, (TOK_DEV, TOK_DEV)))[0:EXTRA, :]
    high = share.astype(BF)
    low = (share - high.astype(F32)).astype(BF)
    tail = jnp.concatenate([high, low], 1)
    grads = grads_ref[...]
    for n, (block, half, w_ref, at) in enumerate(where):
        found = dot_tn(normed_ref[n], grad_value).astype(BF)
        for pair in range(2):
            low_rows = found[pair * 128 : pair * 128 + 64, :]
            high_rows = found[pair * 128 + 64 : (pair + 1) * 128, :]
            owner = block * NX + 2 * half + pair
            kept_ref[owner] = jnp.where(c == 0, low_rows, high_rows)
            given_ref[owner] = jnp.where(c == 0, high_rows, low_rows)
    for i in range(3):
        send(SLOTS + i)
    for n, (block, half, w_ref, at) in enumerate(where):
        terms_ref[block, half, :TOK_DEV, :] = dot_nt(grads, get(w_ref)[at : at + deep, :]).astype(BF)
        terms_ref[block, half, TOK_DEV:, :] = tail
    for k in range(peers):
        put(out_at + k)[...] = terms_ref[lax.rem(peer + k, peers)]
        send(out_at + k)


def finish_kernel(peers, get, put, send, smem, extra):
    hidden_ref, gain_ref, out_ref = get(0), get(1), put(0)
    inverse = get(2)[:, 0:1]
    term_refs = [get(3 + k) for k in range(peers)]
    deep = term_refs[0].shape[2]
    row_dot = None
    for h in range(2):
        total = term_refs[0][h].astype(F32)
        for ref in term_refs[1:]:
            total = total + ref[h].astype(F32)
        if row_dot is None:
            share = total[TOK_DEV : TOK_DEV + 8, :]
            share = share[0:1, :TOK_DEV] + share[0:1, TOK_DEV : 2 * TOK_DEV]
            row_dot = jnp.transpose(jnp.broadcast_to(share, (TOK_DEV, TOK_DEV)))[:, 0:1]
        at = slice(h * deep, (h + 1) * deep)
        weighted = total[:TOK_DEV, :] * gain_ref[:, at].astype(F32)
        here = hidden_ref[:, at].astype(F32)
        out_ref[:, at] = (inverse * weighted - here * (inverse * inverse * inverse * row_dot / D)).astype(BF)


def lay_kernel(get, put, send, smem, extra):
    rows = jnp.concatenate([get(1 + e)[...] for e in range(SLOTS)], 0)
    put(0)[...] = dot_tn(get(0)[...], rows).astype(BF)


def kernel_call(body, outs, args, name, mib, scalars=0, scratch=()):
    shapes = [jax.ShapeDtypeStruct(s, d) for s, d in outs]
    arrays = args[scalars:]
    n_in, n_out = len(arrays), len(shapes)

    def kernel(*refs):
        smem, refs = refs[:scalars], refs[scalars:]
        ins, refs = refs[:n_in], refs[n_in:]
        out, refs = refs[:n_out], refs[n_out:]
        in_buf, refs = refs[:n_in], refs[n_in:]
        out_buf, refs = refs[:n_out], refs[n_out:]
        in_sem, out_sem, extra = refs[0], refs[1], refs[2:]
        loads = [pltpu.make_async_copy(ins[i], in_buf[i], in_sem.at[i]) for i in range(n_in)]
        stores = [pltpu.make_async_copy(out_buf[i], out[i], out_sem.at[i]) for i in range(n_out)]
        for load in loads:
            load.start()
        waited, sent = set(), set()

        def get(i):
            if i not in waited:
                waited.add(i)
                loads[i].wait()
            return in_buf[i]

        def send(i):
            if i not in sent:
                sent.add(i)
                stores[i].start()

        body(get, lambda i: out_buf[i], send, smem, extra)
        for i in range(n_in):
            get(i)
        for i in range(n_out):
            send(i)
        for store in stores:
            store.wait()

    hbm = pl.BlockSpec(memory_space=pltpu.HBM)
    return pl.pallas_call(
        kernel,
        out_shape=shapes,
        in_specs=[pl.BlockSpec(memory_space=pltpu.SMEM)] * scalars + [hbm] * n_in,
        out_specs=[hbm] * n_out,
        scratch_shapes=[pltpu.VMEM(v.shape, v.dtype) for v in arrays]
        + [pltpu.VMEM(v.shape, v.dtype) for v in shapes]
        + [pltpu.SemaphoreType.DMA((n_in,)), pltpu.SemaphoreType.DMA((n_out,))]
        + list(scratch),
        compiler_params=pltpu.CompilerParams(vmem_limit_bytes=mib * MIB),
        name=name,
    )(*args)


def on_device(
    hidden, gain, w_query, w_key, w_value, cotangent, seq_length, home_offset, dest_shard, dest_offset
):
    shards = lax.axis_size("dp")
    peers = lax.axis_size("tensor")
    me, z, x, c = place()
    strides = [-1, 1, shards // 2, shards // 2 + 1]
    width = hidden.shape[1]
    deep = width // 2
    q_cols = w_query.shape[1]
    k_cols = w_key.shape[1]
    q_heads = q_cols // HEAD
    rows_each = D // shards

    own = jnp.concatenate([w_query, w_key, w_value], 1)
    slab = lax.all_gather(
        own, "dp", axis=0, tiled=True,
        axis_index_groups=[[a * NX * NC + b for b in range(NX * NC)] for a in range(NZ)],
    )
    first = jnp.where(c == 0, slab[:deep], slab[deep:])
    second = jnp.where(c == 0, slab[deep:], slab[:deep])

    half = HEAD // 2
    freq = np.power(np.float32(ROPE_BASE), -(np.arange(half, dtype=np.float32) * np.float32(2.0 / HEAD)))
    freq = jnp.asarray(np.concatenate([freq, freq])[None, :].astype(np.float32))
    square = ((TOK_DEV, TOK_DEV), F32)
    cut = ((MAXLEN, q_cols), BF)
    slab, cotangent = tied(slab, cotangent)
    *cot_cuts, home, dest, cosine, sine, allowed = kernel_call(
        functools.partial(plan_kernel, strides, shards),
        [cut] * 4 + [((SLOTS * MAXLEN, TOK_DEV), BF), ((SLOTS * MAXLEN, CAP), BF)] + [square] * 3,
        [seq_length.T, home_offset.T, dest_shard.T, dest_offset.T, freq, cotangent],
        "plan", 60, 4,
    )
    packed = jnp.concatenate([hidden, jnp.broadcast_to(gain[None, :], (EXTRA, width))], 0)
    packed = packed.reshape(TOK_DEV + EXTRA, 2, deep).transpose(1, 0, 2)
    packed = jnp.broadcast_to(packed[None], (peers,) + packed.shape)

    def sent_home(n):
        return passed_along(cot_cuts[n], -strides[n])

    weights, cots = [slab], []
    first, second, *landed, packed = tied(
        along_z(first), along_z(second), sent_home(0), sent_home(1), sent_home(2), packed
    )
    cots += landed
    rows_full = lax.all_to_all(packed, "tensor", split_axis=0, concat_axis=0, tiled=True)
    weights += [first, second]
    first, second, *landed = tied(
        along_z(first), along_z(second), other_core(first), other_core(second)
    )
    weights += landed + [first, second]
    first, second, *landed = tied(
        along_z(first), along_z(second), other_core(first), other_core(second)
    )
    weights += landed + [first, second]
    first, *landed, last = tied(
        along_z(first), other_core(first), other_core(second), sent_home(3)
    )
    cots.append(last)
    weights += landed + [first, other_core(first)]

    pieces = len(weights)
    share = ((NZ * NX, rows_each, k_cols), BF)
    block = ((2, TOK_DEV + EXTRA, deep), BF)
    *attn_cuts, kept, given, inverse, t0, t1, t2, t3, t4, t5, t6, t7 = kernel_call(
        functools.partial(layer_kernel, q_heads, pieces, peers),
        [cut] * 4 + [share, share, square] + [block] * peers,
        [rows_full, cosine, sine, allowed, home, *cots, *weights],
        "layer", 60, 0,
        [
            pltpu.VMEM((2 * NZ, TOK_DEV, deep), BF),
            pltpu.VMEM((TOK_DEV, q_cols + 2 * k_cols), BF),
            pltpu.VMEM((peers, 2, TOK_DEV + EXTRA, deep), BF),
        ],
    )

    pair = (kept.astype(F32) + other_core(given).astype(F32)).astype(BF)
    terms = [t0] + [
        lax.ppermute(t, "tensor", [(i, (i + k) % peers) for i in range(peers)])
        for k, t in enumerate((t1, t2, t3, t4, t5, t6, t7), 1)
    ]
    terms[1], terms[2], pair, *attn_cuts = tied(terms[1], terms[2], pair, *attn_cuts)
    parts = lax.all_to_all(
        pair, "dp", split_axis=0, concat_axis=0, tiled=True,
        axis_index_groups=[list(range(b, shards, NC)) for b in range(NC)],
    )
    grad_value_weight = jnp.sum(parts.astype(F32), 0)
    (grad_hidden,) = kernel_call(
        functools.partial(finish_kernel, peers), [((TOK_DEV, width), BF)],
        [hidden, gain[None, :], inverse, *terms], "finish", 8,
    )
    attn_sent = [passed_along(attn_cuts[n], s) for n, s in enumerate(strides)]
    (attn_out,) = kernel_call(lay_kernel, [((CAP, q_cols), BF)], [dest, *attn_sent], "lay", 8)
    return (attn_out, grad_hidden, grad_value_weight)


def solution(mesh):
    return jax.shard_map(
        on_device,
        mesh=mesh,
        in_specs=(P("dp", "tensor"), P("tensor")) + (P("dp", "tensor"),) * 4 + (P(),) * 4,
        out_specs=(P("dp", "tensor"), P("dp", "tensor"), P("dp", "tensor")),
        check_vma=False,
    )
```

```python
import functools

import jax
import jax.numpy as jnp
import numpy as np
from jax import lax
from jax.experimental import pallas as pl
from jax.experimental.pallas import tpu as pltpu
from jax.sharding import Mesh, PartitionSpec as P

D = 4096
HEAD = 128
TOK_DEV = 128
MAXLEN = 64
CAP = 256
SLOTS = 4
EXTRA = 16
EPSILON = 1e-05
ROPE_BASE = 500000.0
NZ, NX, NC = 8, 4, 2
DP = ("z", "x", "core")
BF = jnp.bfloat16
F32 = jnp.float32
MIB = 1024 * 1024


def moved(value, where):
    pairs = []
    for z in range(NZ):
        for x in range(NX):
            for c in range(NC):
                tz, tx, tc = where(z, x, c)
                pairs.append(((z * NX + x) * NC + c, ((tz % NZ) * NX + tx % NX) * NC + tc))
    return lax.ppermute(value, DP, pairs)


def other_core(value):
    return moved(value, lambda z, x, c: (z, x, 1 - c))


def passed_along(value, by):
    size = NZ * NX * NC
    return lax.ppermute(value, DP, [(i, (i + by) % size) for i in range(size)])


def tied(*values):
    return lax.optimization_barrier(values)


def dot_nn(a, b):
    return lax.dot_general(a, b, (((1,), (0,)), ((), ())), preferred_element_type=F32)


def dot_nt(a, b):
    return lax.dot_general(a, b, (((1,), (1,)), ((), ())), preferred_element_type=F32)


def dot_tn(a, b):
    return lax.dot_general(a, b, (((0,), (0,)), ((), ())), preferred_element_type=F32)


def place():
    z, x, c = [lax.axis_index(axis) for axis in DP]
    return (z * NX + x) * NC + c, z, x, c


def plan_kernel(
    strides, shards, get, put, send, smem, extra,
):
    len_ref, off_ref, shard_ref, start_ref = smem
    home_ref, dest_ref, cos_ref, sin_ref, allowed_ref = [put(3 + i) for i in range(5)]
    me = place()[0]
    rows = lax.broadcasted_iota(jnp.int32, (TOK_DEV, TOK_DEV), 0)
    cols = lax.broadcasted_iota(jnp.int32, (TOK_DEV, TOK_DEV), 1)
    row_seq, row_pos = jnp.zeros_like(rows), jnp.zeros_like(rows)
    col_seq, col_pos = jnp.zeros_like(rows), jnp.zeros_like(rows)
    for e, stride in enumerate(strides):
        target = lax.rem(me + stride + shards, shards)
        source = lax.rem(me - stride + shards, shards)
        length = jnp.int32(0)
        offset = jnp.int32(0)
        in_len = jnp.int32(0)
        in_start = jnp.int32(0)
        for c in range(SLOTS):
            mine = shard_ref[c, me] == target
            length = length + jnp.where(mine, len_ref[c, me], 0)
            offset = offset + jnp.where(mine, off_ref[c, me], 0)
            theirs = shard_ref[c, source] == me
            in_len = in_len + jnp.where(theirs, len_ref[c, source], 0)
            in_start = in_start + jnp.where(theirs, start_ref[c, source], 0)
        inside = (rows >= offset) & (rows < offset + length)
        row_seq = jnp.where(inside, e, row_seq)
        row_pos = jnp.where(inside, rows - offset, row_pos)
        inside = (cols >= offset) & (cols < offset + length)
        col_seq = jnp.where(inside, e, col_seq)
        col_pos = jnp.where(inside, cols - offset, col_pos)
        at = slice(e * MAXLEN, (e + 1) * MAXLEN)
        t = lax.broadcasted_iota(jnp.int32, (MAXLEN, TOK_DEV), 0)
        r = lax.broadcasted_iota(jnp.int32, (MAXLEN, TOK_DEV), 1)
        home_ref[at, :] = jnp.where((r == t + offset) & (t < length), 1.0, 0.0).astype(BF)
        t = lax.broadcasted_iota(jnp.int32, (MAXLEN, CAP), 0)
        r = lax.broadcasted_iota(jnp.int32, (MAXLEN, CAP), 1)
        dest = jnp.where((r == t + in_start) & (t < in_len), 1.0, 0.0).astype(BF)
        dest_ref[at, :] = dest
        ref, lo = ((1, 0), (0, 0), (2, 0), (0, MAXLEN))[e]
        put(ref)[lo : lo + MAXLEN, :] = dot_nn(dest, get(1)[...]).astype(BF)
    allowed_ref[...] = jnp.where((row_seq == col_seq) & (col_pos <= row_pos), 1.0, 0.0)
    angles = row_pos.astype(F32) * get(0)[...]
    cos_ref[...] = jnp.cos(angles)
    sine = jnp.sin(angles)
    sin_ref[...] = jnp.where(cols < HEAD // 2, -sine, sine)


def layer_kernel(q_heads, get, put, send, smem, extra):
    normed_ref, grads_ref = extra
    kept_ref, given_ref, inverse_ref, terms_ref = [put(3 + i) for i in range(4)]
    _, z, x, c = place()
    where = [(j, h, ref, j * 256) for j in range(NZ) for h, ref in ((c, 8), (1 - c, 9))]
    rows_ref = get(0)
    deep = rows_ref.shape[3]
    kv_at = q_heads * HEAD
    squares = jnp.zeros((TOK_DEV, 1), F32)
    for j in range(NZ):
        for h in range(2):
            part = rows_ref[j, h, :TOK_DEV, :].astype(F32)
            squares = squares + jnp.sum(part * part, 1, keepdims=True)
    inverse = lax.rsqrt(squares / D + EPSILON)
    inverse_ref[...] = jnp.broadcast_to(inverse, inverse_ref.shape)
    projected = jnp.zeros((TOK_DEV, kv_at + 2 * HEAD), F32)
    for n, (block, half, w_ref, at) in enumerate(where):
        gain = rows_ref[block, half, TOK_DEV:, :].astype(F32)[0:1, :]
        part = (rows_ref[block, half, :TOK_DEV, :].astype(F32) * inverse * gain).astype(BF)
        normed_ref[n] = part
        projected = projected + dot_nn(part, get(w_ref)[at : at + deep, :])
    cosine = get(1)[...]
    sine = get(2)[...]
    factor = HEAD ** (-0.5)
    allowed = get(3)[...] > 0.5
    home = get(4)[...]
    cot = jnp.concatenate(
        [get(6)[...], get(5)[:MAXLEN, :], get(7)[...]], 0
    )
    cot = dot_tn(home, cot).astype(BF)
    key_raw = projected[:, kv_at : kv_at + HEAD]
    value_raw = projected[:, kv_at + HEAD :]
    key = (key_raw * cosine + pltpu.roll(key_raw, HEAD // 2, 1) * sine).astype(BF)
    value = value_raw.astype(BF)
    grad_key = jnp.zeros((TOK_DEV, HEAD), F32)
    grad_value = jnp.zeros((TOK_DEV, HEAD), F32)
    dots = jnp.zeros((TOK_DEV, HEAD), F32)
    for g in range(q_heads):
        at = slice(g * HEAD, (g + 1) * HEAD)
        query_raw = projected[:, at]
        query = (query_raw * cosine + pltpu.roll(query_raw, HEAD // 2, 1) * sine).astype(BF)
        scores = jnp.where(allowed, dot_nt(query, key) * factor, F32(-1e30))
        exp_terms = jnp.exp(scores - jnp.max(scores, -1, keepdims=True))
        probs = exp_terms / jnp.sum(exp_terms, -1, keepdims=True)
        probs_low = probs.astype(BF)
        mixed = dot_nn(probs_low, value).astype(BF)
        mixed = dot_nn(home, mixed).astype(BF)
        put(0)[:, at] = mixed[:MAXLEN, :]
        put(1)[:, at] = mixed[MAXLEN : 2 * MAXLEN, :]
        put(2)[:, at] = mixed[2 * MAXLEN :, :]
        grad_out = cot[:, at]
        grad_value = grad_value + dot_tn(probs_low, grad_out)
        grad_probs = dot_nt(grad_out, value)
        centre = jnp.sum(grad_probs * probs, -1, keepdims=True)
        grad_scores = (probs * (grad_probs - centre) * factor).astype(BF)
        grad_query = dot_nn(grad_scores, key)
        grad_key = grad_key + dot_tn(grad_scores, query)
        grad_query = (grad_query * cosine - pltpu.roll(grad_query, HEAD // 2, 1) * sine).astype(BF)
        grads_ref[:, at] = grad_query
        dots = dots + grad_query.astype(F32) * query_raw
    grad_key = (grad_key * cosine - pltpu.roll(grad_key, HEAD // 2, 1) * sine).astype(BF)
    grad_value = grad_value.astype(BF)
    grads_ref[:, kv_at : kv_at + HEAD] = grad_key
    grads_ref[:, kv_at + HEAD :] = grad_value
    dots = dots + grad_key.astype(F32) * key_raw + grad_value.astype(F32) * value_raw
    for i in range(3):
        send(i)
    share = jnp.sum(dots, 1, keepdims=True) / inverse
    share = jnp.transpose(jnp.broadcast_to(share, (TOK_DEV, TOK_DEV)))[0:EXTRA, :]
    high = share.astype(BF)
    low = (share - high.astype(F32)).astype(BF)
    tail = jnp.concatenate([high, low], 1)
    grads = grads_ref[...]
    for n, (block, half, w_ref, at) in enumerate(where):
        found = dot_tn(normed_ref[n], grad_value).astype(BF)
        for pair in range(2):
            low_rows = found[pair * 128 : pair * 128 + 64, :]
            high_rows = found[pair * 128 + 64 : (pair + 1) * 128, :]
            owner = block * NX + 2 * half + pair
            kept_ref[owner] = jnp.where(c == 0, low_rows, high_rows)
            given_ref[owner] = jnp.where(c == 0, high_rows, low_rows)
    for i in range(3):
        send(3 + i)
    for n, (block, half, w_ref, at) in enumerate(where):
        terms_ref[block, half, :TOK_DEV, :] = dot_nt(grads, get(w_ref)[at : at + deep, :]).astype(BF)
        terms_ref[block, half, TOK_DEV:, :] = tail


def finish_kernel(get, put, send, smem, extra):
    hidden_ref, gain_ref, total_ref, out_ref = get(0), get(1), get(3), put(0)
    inverse = get(2)[:, 0:1]
    deep = total_ref.shape[2]
    share = total_ref[0, TOK_DEV:, :].astype(F32)
    share = share[0:1, :TOK_DEV] + share[0:1, TOK_DEV : 2 * TOK_DEV]
    row_dot = jnp.transpose(jnp.broadcast_to(share, (TOK_DEV, TOK_DEV)))[:, 0:1]
    for h in range(2):
        at = slice(h * deep, (h + 1) * deep)
        weighted = total_ref[h, :TOK_DEV, :].astype(F32) * gain_ref[:, at].astype(F32)
        here = hidden_ref[:, at].astype(F32)
        out_ref[:, at] = (inverse * weighted - here * (inverse * inverse * inverse * row_dot / D)).astype(BF)


def lay_kernel(get, put, send, smem, extra):
    rows = jnp.concatenate(
        [get(1)[...], get(2)[:MAXLEN, :], get(3)[...], get(2)[MAXLEN:, :]], 0
    )
    put(0)[...] = dot_tn(get(0)[...], rows).astype(BF)


def kernel_call(body, outs, args, name, mib, scalars=0, scratch=()):
    shapes = [jax.ShapeDtypeStruct(s, d) for s, d in outs]
    arrays = args[scalars:]
    n_in, n_out = len(arrays), len(shapes)

    def kernel(*refs):
        smem, refs = refs[:scalars], refs[scalars:]
        ins, refs = refs[:n_in], refs[n_in:]
        out, refs = refs[:n_out], refs[n_out:]
        in_buf, refs = refs[:n_in], refs[n_in:]
        out_buf, refs = refs[:n_out], refs[n_out:]
        in_sem, out_sem, extra = refs[0], refs[1], refs[2:]
        loads = [pltpu.make_async_copy(ins[i], in_buf[i], in_sem.at[i]) for i in range(n_in)]
        stores = [pltpu.make_async_copy(out_buf[i], out[i], out_sem.at[i]) for i in range(n_out)]
        for load in loads:
            load.start()
        waited, sent = set(), set()

        def get(i):
            if i not in waited:
                waited.add(i)
                loads[i].wait()
            return in_buf[i]

        def send(i):
            if i not in sent:
                sent.add(i)
                stores[i].start()

        body(get, lambda i: out_buf[i], send, smem, extra)
        for i in range(n_in):
            get(i)
        for i in range(n_out):
            send(i)
        for store in stores:
            store.wait()

    hbm = pl.BlockSpec(memory_space=pltpu.HBM)
    return pl.pallas_call(
        kernel,
        out_shape=shapes,
        in_specs=[pl.BlockSpec(memory_space=pltpu.SMEM)] * scalars + [hbm] * n_in,
        out_specs=[hbm] * n_out,
        scratch_shapes=[pltpu.VMEM(v.shape, v.dtype) for v in arrays]
        + [pltpu.VMEM(v.shape, v.dtype) for v in shapes]
        + [pltpu.SemaphoreType.DMA((n_in,)), pltpu.SemaphoreType.DMA((n_out,))]
        + list(scratch),
        compiler_params=pltpu.CompilerParams(vmem_limit_bytes=mib * MIB),
        name=name,
    )(*args)


def on_device(
    hidden, gain, w_query, w_key, w_value, cotangent, seq_length, home_offset, dest_shard, dest_offset
):
    shards = NZ * NX * NC
    peers = lax.axis_size("tensor")
    me, z, x, c = place()
    strides = [-1, 1, shards // 2, shards // 2 + 1]
    width = hidden.shape[1]
    deep = width // 2
    q_cols = w_query.shape[1]
    k_cols = w_key.shape[1]
    q_heads = q_cols // HEAD
    rows_each = D // shards

    own = jnp.concatenate([w_query, w_key, w_value], 1)
    slab = lax.all_gather(own, ("x", "core"), axis=0, tiled=True)
    own_half = jnp.where(c == 0, slab[:deep], slab[deep:])
    own_half, cotangent, packed = tied(own_half, cotangent, hidden)
    mine = lax.all_gather(own_half, "z", axis=0, tiled=True)

    half = HEAD // 2
    freq = np.power(np.float32(ROPE_BASE), -(np.arange(half, dtype=np.float32) * np.float32(2.0 / HEAD)))
    freq = jnp.asarray(np.concatenate([freq, freq])[None, :].astype(np.float32))
    square = ((TOK_DEV, TOK_DEV), F32)
    cut = ((MAXLEN, q_cols), BF)
    wide = ((2 * MAXLEN, q_cols), BF)
    cot_near, cot_behind, cot_far, home, dest, cosine, sine, allowed = kernel_call(
        functools.partial(plan_kernel, strides, shards),
        [wide, cut, cut] + [((SLOTS * MAXLEN, TOK_DEV), BF), ((SLOTS * MAXLEN, CAP), BF)] + [square] * 3,
        [seq_length.T, home_offset.T, dest_shard.T, dest_offset.T, freq, cotangent],
        "plan", 60, 4,
    )
    packed = jnp.concatenate([packed, jnp.broadcast_to(gain[None, :], (EXTRA, width))], 0)
    packed = packed.reshape(TOK_DEV + EXTRA, 2, deep).transpose(1, 0, 2)
    packed = jnp.broadcast_to(packed[None], (peers,) + packed.shape)

    rows_full = lax.all_to_all(packed, "tensor", split_axis=0, concat_axis=0, tiled=True)
    cot_near = passed_along(cot_near, -1)
    cot_behind = passed_along(cot_behind, 1)
    cot_far = passed_along(jnp.concatenate([cot_far, cot_near[MAXLEN:]], 0), shards // 2)

    mine, rows_full, cot_near, cot_behind, cot_far = tied(
        mine, rows_full, cot_near, cot_behind, cot_far
    )
    theirs = other_core(mine)

    share = ((NZ * NX, rows_each, k_cols), BF)
    block = (2, TOK_DEV + EXTRA, deep)
    attn_behind, attn_near, attn_far, kept, given, inverse, terms = kernel_call(
        functools.partial(layer_kernel, q_heads),
        [cut, cut, wide, share, share, square, ((peers,) + block, BF)],
        [rows_full, cosine, sine, allowed, home, cot_near, cot_behind, cot_far, mine, theirs],
        "layer", 60, 0,
        [
            pltpu.VMEM((2 * NZ, TOK_DEV, deep), BF),
            pltpu.VMEM((TOK_DEV, q_cols + 2 * k_cols), BF),
        ],
    )
    total = lax.psum_scatter(terms, "tensor", scatter_dimension=0, tiled=False)
    (grad_hidden,) = kernel_call(
        finish_kernel, [((TOK_DEV, width), BF)],
        [hidden, gain[None, :], inverse, total], "finish", 8,
    )

    pair = (kept.astype(F32) + other_core(given).astype(F32)).astype(BF)
    parts = lax.all_to_all(pair, ("z", "x"), split_axis=0, concat_axis=0, tiled=True)
    grad_value_weight = jnp.sum(parts.astype(F32), 0)

    attn_far = passed_along(attn_far, shards // 2)
    attn_near = passed_along(jnp.concatenate([attn_near, attn_far[MAXLEN:]], 0), 1)
    attn_behind = passed_along(attn_behind, -1)
    (attn_out,) = kernel_call(
        lay_kernel, [((CAP, q_cols), BF)], [dest, attn_behind, attn_near, attn_far[:MAXLEN]], "lay", 8
    )
    return (attn_out, grad_hidden, grad_value_weight)


def solution(mesh):
    fine = Mesh(mesh.devices.reshape(NZ, NX, NC, -1), DP + ("tensor",))
    both = P(DP, "tensor")
    return jax.shard_map(
        on_device,
        mesh=fine,
        in_specs=(both, P("tensor")) + (both,) * 4 + (P(),) * 4,
        out_specs=(both,) * 3,
        check_vma=False,
    )
```

```python
import functools

import jax
import jax.numpy as jnp
import numpy as np
from jax import lax
from jax.experimental import pallas as pl
from jax.experimental.pallas import tpu as pltpu
from jax.sharding import Mesh, PartitionSpec as P

D = 4096
HEAD = 128
TOK_DEV = 128
MAXLEN = 64
CAP = 256
SLOTS = 4
EXTRA = 16
EPSILON = 1e-05
ROPE_BASE = 500000.0
NZ, NX, NC = 8, 4, 2
DP = ("z", "x", "core")
BF = jnp.bfloat16
F32 = jnp.float32
MIB = 1024 * 1024


def moved(value, where):
    pairs = []
    for z in range(NZ):
        for x in range(NX):
            for c in range(NC):
                tz, tx, tc = where(z, x, c)
                pairs.append(((z * NX + x) * NC + c, ((tz % NZ) * NX + tx % NX) * NC + tc))
    return lax.ppermute(value, DP, pairs)


def other_core(value):
    return moved(value, lambda z, x, c: (z, x, 1 - c))


def passed_along(value, by):
    size = NZ * NX * NC
    return lax.ppermute(value, DP, [(i, (i + by) % size) for i in range(size)])


def tied(*values):
    return lax.optimization_barrier(values)


def dot_nn(a, b):
    return lax.dot_general(a, b, (((1,), (0,)), ((), ())), preferred_element_type=F32)


def dot_nt(a, b):
    return lax.dot_general(a, b, (((1,), (1,)), ((), ())), preferred_element_type=F32)


def dot_tn(a, b):
    return lax.dot_general(a, b, (((0,), (0,)), ((), ())), preferred_element_type=F32)


def place():
    z, x, c = [lax.axis_index(axis) for axis in DP]
    return (z * NX + x) * NC + c, z, x, c


def plan_kernel(
    strides, shards, get, put, send, smem, extra,
):
    len_ref, off_ref, shard_ref, start_ref = smem
    home_ref, dest_ref, cos_ref, sin_ref, allowed_ref = [put(3 + i) for i in range(5)]
    me = place()[0]
    rows = lax.broadcasted_iota(jnp.int32, (TOK_DEV, TOK_DEV), 0)
    cols = lax.broadcasted_iota(jnp.int32, (TOK_DEV, TOK_DEV), 1)
    row_seq, row_pos = jnp.zeros_like(rows), jnp.zeros_like(rows)
    col_seq, col_pos = jnp.zeros_like(rows), jnp.zeros_like(rows)
    for e, stride in enumerate(strides):
        target = lax.rem(me + stride + shards, shards)
        source = lax.rem(me - stride + shards, shards)
        length = jnp.int32(0)
        offset = jnp.int32(0)
        in_len = jnp.int32(0)
        in_start = jnp.int32(0)
        for c in range(SLOTS):
            mine = shard_ref[c, me] == target
            length = length + jnp.where(mine, len_ref[c, me], 0)
            offset = offset + jnp.where(mine, off_ref[c, me], 0)
            theirs = shard_ref[c, source] == me
            in_len = in_len + jnp.where(theirs, len_ref[c, source], 0)
            in_start = in_start + jnp.where(theirs, start_ref[c, source], 0)
        inside = (rows >= offset) & (rows < offset + length)
        row_seq = jnp.where(inside, e, row_seq)
        row_pos = jnp.where(inside, rows - offset, row_pos)
        inside = (cols >= offset) & (cols < offset + length)
        col_seq = jnp.where(inside, e, col_seq)
        col_pos = jnp.where(inside, cols - offset, col_pos)
        at = slice(e * MAXLEN, (e + 1) * MAXLEN)
        t = lax.broadcasted_iota(jnp.int32, (MAXLEN, TOK_DEV), 0)
        r = lax.broadcasted_iota(jnp.int32, (MAXLEN, TOK_DEV), 1)
        home_ref[at, :] = jnp.where((r == t + offset) & (t < length), 1.0, 0.0).astype(BF)
        t = lax.broadcasted_iota(jnp.int32, (MAXLEN, CAP), 0)
        r = lax.broadcasted_iota(jnp.int32, (MAXLEN, CAP), 1)
        dest = jnp.where((r == t + in_start) & (t < in_len), 1.0, 0.0).astype(BF)
        dest_ref[at, :] = dest
        ref, lo = ((1, 0), (0, 0), (2, 0), (0, MAXLEN))[e]
        put(ref)[lo : lo + MAXLEN, :] = dot_nn(dest, get(1)[...]).astype(BF)
    allowed_ref[...] = jnp.where((row_seq == col_seq) & (col_pos <= row_pos), 1.0, 0.0)
    angles = row_pos.astype(F32) * get(0)[...]
    cos_ref[...] = jnp.cos(angles)
    sine = jnp.sin(angles)
    sin_ref[...] = jnp.where(cols < HEAD // 2, -sine, sine)


def norm_kernel(get, put, send, smem, extra):
    c = place()[3]
    rows_ref, normed_ref, inverse_ref, partial_ref = get(0), put(0), put(1), put(2)
    deep = rows_ref.shape[3]
    squares = jnp.zeros((TOK_DEV, 1), F32)
    for j in range(NZ):
        for h in range(2):
            part = rows_ref[j, h, :TOK_DEV, :].astype(F32)
            squares = squares + jnp.sum(part * part, 1, keepdims=True)
    inverse = lax.rsqrt(squares / D + EPSILON)
    inverse_ref[...] = jnp.broadcast_to(inverse, inverse_ref.shape)
    for n, half in enumerate((c, 1 - c)):
        for j in range(NZ):
            gain = rows_ref[j, half, TOK_DEV:, :].astype(F32)[0:1, :]
            part = rows_ref[j, half, :TOK_DEV, :].astype(F32) * inverse * gain
            normed_ref[n, j] = part.astype(BF)
    send(0)
    partial = jnp.zeros(partial_ref.shape, F32)
    for j in range(NZ):
        partial = partial + dot_nn(normed_ref[0, j], get(1)[j * deep : (j + 1) * deep, :])
    partial_ref[...] = partial


def value_kernel(get, put, send, smem, extra):
    c = place()[3]
    kept_ref, given_ref = put(0), put(1)
    grad_value = get(1)[...]
    for n, half in enumerate((c, 1 - c)):
        for j in range(NZ):
            found = dot_tn(get(0)[n, j], grad_value).astype(BF)
            for pair in range(2):
                low_rows = found[pair * 128 : pair * 128 + 64, :]
                high_rows = found[pair * 128 + 64 : (pair + 1) * 128, :]
                owner = j * NX + 2 * half + pair
                kept_ref[owner] = jnp.where(c == 0, low_rows, high_rows)
                given_ref[owner] = jnp.where(c == 0, high_rows, low_rows)


def layer_kernel(q_heads, get, put, send, smem, extra):
    (grads_ref,) = extra
    value_out_ref, terms_ref = put(4), put(5)
    c = place()[3]
    kv_at = q_heads * HEAD
    inverse = get(9)[:, 0:1]
    normed_ref = get(0)
    deep = normed_ref.shape[3]
    projected = get(10)[...]
    for j in range(NZ):
        projected = projected + dot_nn(normed_ref[1, j], get(11)[j * deep : (j + 1) * deep, :])
    cosine = get(1)[...]
    sine = get(2)[...]
    factor = HEAD ** (-0.5)
    allowed = get(3)[...] > 0.5
    home = get(4)[...]
    cot = jnp.concatenate(
        [get(6)[...], get(5)[:MAXLEN, :], get(7)[...]], 0
    )
    cot = dot_tn(home, cot).astype(BF)
    key_raw = projected[:, kv_at : kv_at + HEAD]
    value_raw = projected[:, kv_at + HEAD :]
    key = (key_raw * cosine + pltpu.roll(key_raw, HEAD // 2, 1) * sine).astype(BF)
    value = value_raw.astype(BF)
    grad_key = jnp.zeros((TOK_DEV, HEAD), F32)
    grad_value = jnp.zeros((TOK_DEV, HEAD), F32)
    dots = jnp.zeros((TOK_DEV, HEAD), F32)
    for g in range(q_heads):
        at = slice(g * HEAD, (g + 1) * HEAD)
        query_raw = projected[:, at]
        query = (query_raw * cosine + pltpu.roll(query_raw, HEAD // 2, 1) * sine).astype(BF)
        scores = jnp.where(allowed, dot_nt(query, key) * factor, F32(-1e30))
        exp_terms = jnp.exp(scores - jnp.max(scores, -1, keepdims=True))
        probs = exp_terms / jnp.sum(exp_terms, -1, keepdims=True)
        probs_low = probs.astype(BF)
        mixed = dot_nn(probs_low, value).astype(BF)
        mixed = dot_nn(home, mixed).astype(BF)
        for e in range(SLOTS):
            put(e)[:, at] = mixed[e * MAXLEN : (e + 1) * MAXLEN, :]
        grad_out = cot[:, at]
        grad_value = grad_value + dot_tn(probs_low, grad_out)
        grad_probs = dot_nt(grad_out, value)
        centre = jnp.sum(grad_probs * probs, -1, keepdims=True)
        grad_scores = (probs * (grad_probs - centre) * factor).astype(BF)
        grad_query = dot_nn(grad_scores, key)
        grad_key = grad_key + dot_tn(grad_scores, query)
        grad_query = (grad_query * cosine - pltpu.roll(grad_query, HEAD // 2, 1) * sine).astype(BF)
        grads_ref[:, at] = grad_query
        dots = dots + grad_query.astype(F32) * query_raw
    grad_key = (grad_key * cosine - pltpu.roll(grad_key, HEAD // 2, 1) * sine).astype(BF)
    grad_value = grad_value.astype(BF)
    grads_ref[:, kv_at : kv_at + HEAD] = grad_key
    grads_ref[:, kv_at + HEAD :] = grad_value
    value_out_ref[...] = grad_value
    dots = dots + grad_key.astype(F32) * key_raw + grad_value.astype(F32) * value_raw
    for e in range(SLOTS):
        send(e)
    share = jnp.sum(dots, 1, keepdims=True) / inverse
    share = jnp.transpose(jnp.broadcast_to(share, (TOK_DEV, TOK_DEV)))[0:EXTRA, :]
    high = share.astype(BF)
    low = (share - high.astype(F32)).astype(BF)
    tail = jnp.concatenate([high, low], 1)
    grads = grads_ref[...]
    for half, ref in ((c, 8), (1 - c, 11)):
        for j in range(NZ):
            found = dot_nt(grads, get(ref)[j * deep : (j + 1) * deep, :])
            terms_ref[j, half, :TOK_DEV, :] = found.astype(BF)
            terms_ref[j, half, TOK_DEV:, :] = tail


def finish_kernel(get, put, send, smem, extra):
    hidden_ref, gain_ref, total_ref, out_ref = get(0), get(1), get(3), put(0)
    inverse = get(2)[:, 0:1]
    deep = total_ref.shape[2]
    share = total_ref[0, TOK_DEV:, :].astype(F32)
    share = share[0:1, :TOK_DEV] + share[0:1, TOK_DEV : 2 * TOK_DEV]
    row_dot = jnp.transpose(jnp.broadcast_to(share, (TOK_DEV, TOK_DEV)))[:, 0:1]
    for h in range(2):
        at = slice(h * deep, (h + 1) * deep)
        weighted = total_ref[h, :TOK_DEV, :].astype(F32) * gain_ref[:, at].astype(F32)
        here = hidden_ref[:, at].astype(F32)
        out_ref[:, at] = (inverse * weighted - here * (inverse * inverse * inverse * row_dot / D)).astype(BF)


def lay_kernel(get, put, send, smem, extra):
    rows = jnp.concatenate(
        [get(1 + e)[...] for e in range(SLOTS)], 0
    )
    put(0)[...] = dot_tn(get(0)[...], rows).astype(BF)


def kernel_call(body, outs, args, name, mib, scalars=0, scratch=()):
    shapes = [jax.ShapeDtypeStruct(s, d) for s, d in outs]
    arrays = args[scalars:]
    n_in, n_out = len(arrays), len(shapes)

    def kernel(*refs):
        smem, refs = refs[:scalars], refs[scalars:]
        ins, refs = refs[:n_in], refs[n_in:]
        out, refs = refs[:n_out], refs[n_out:]
        in_buf, refs = refs[:n_in], refs[n_in:]
        out_buf, refs = refs[:n_out], refs[n_out:]
        in_sem, out_sem, extra = refs[0], refs[1], refs[2:]
        loads = [pltpu.make_async_copy(ins[i], in_buf[i], in_sem.at[i]) for i in range(n_in)]
        stores = [pltpu.make_async_copy(out_buf[i], out[i], out_sem.at[i]) for i in range(n_out)]
        for load in loads:
            load.start()
        waited, sent = set(), set()

        def get(i):
            if i not in waited:
                waited.add(i)
                loads[i].wait()
            return in_buf[i]

        def send(i):
            if i not in sent:
                sent.add(i)
                stores[i].start()

        body(get, lambda i: out_buf[i], send, smem, extra)
        for i in range(n_in):
            get(i)
        for i in range(n_out):
            send(i)
        for store in stores:
            store.wait()

    hbm = pl.BlockSpec(memory_space=pltpu.HBM)
    return pl.pallas_call(
        kernel,
        out_shape=shapes,
        in_specs=[pl.BlockSpec(memory_space=pltpu.SMEM)] * scalars + [hbm] * n_in,
        out_specs=[hbm] * n_out,
        scratch_shapes=[pltpu.VMEM(v.shape, v.dtype) for v in arrays]
        + [pltpu.VMEM(v.shape, v.dtype) for v in shapes]
        + [pltpu.SemaphoreType.DMA((n_in,)), pltpu.SemaphoreType.DMA((n_out,))]
        + list(scratch),
        compiler_params=pltpu.CompilerParams(vmem_limit_bytes=mib * MIB),
        name=name,
    )(*args)


def on_device(
    hidden, gain, w_query, w_key, w_value, cotangent, seq_length, home_offset, dest_shard, dest_offset
):
    shards = NZ * NX * NC
    peers = lax.axis_size("tensor")
    me, z, x, c = place()
    strides = [-1, 1, shards // 2, shards // 2 + 1]
    width = hidden.shape[1]
    deep = width // 2
    q_cols = w_query.shape[1]
    k_cols = w_key.shape[1]
    q_heads = q_cols // HEAD
    rows_each = D // shards

    own = jnp.concatenate([w_query, w_key, w_value], 1)
    slab = lax.all_gather(own, ("x", "core"), axis=0, tiled=True)
    own_half = jnp.where(c == 0, slab[:deep], slab[deep:])
    own_half, cotangent, packed = tied(own_half, cotangent, hidden)
    mine = lax.all_gather(own_half, "z", axis=0, tiled=True)

    half = HEAD // 2
    freq = np.power(np.float32(ROPE_BASE), -(np.arange(half, dtype=np.float32) * np.float32(2.0 / HEAD)))
    freq = jnp.asarray(np.concatenate([freq, freq])[None, :].astype(np.float32))
    square = ((TOK_DEV, TOK_DEV), F32)
    cut = ((MAXLEN, q_cols), BF)
    wide = ((2 * MAXLEN, q_cols), BF)
    cot_near, cot_behind, cot_far, home, dest, cosine, sine, allowed = kernel_call(
        functools.partial(plan_kernel, strides, shards),
        [wide, cut, cut] + [((SLOTS * MAXLEN, TOK_DEV), BF), ((SLOTS * MAXLEN, CAP), BF)] + [square] * 3,
        [seq_length.T, home_offset.T, dest_shard.T, dest_offset.T, freq, cotangent],
        "plan", 60, 4,
    )
    packed = jnp.concatenate([packed, jnp.broadcast_to(gain[None, :], (EXTRA, width))], 0)
    packed = packed.reshape(TOK_DEV + EXTRA, 2, deep).transpose(1, 0, 2)
    packed = jnp.broadcast_to(packed[None], (peers,) + packed.shape)

    rows_full = lax.all_to_all(packed, "tensor", split_axis=0, concat_axis=0, tiled=True)
    cot_near = passed_along(cot_near, -1)
    cot_behind = passed_along(cot_behind, 1)
    cot_far = passed_along(jnp.concatenate([cot_far, cot_near[MAXLEN:]], 0), shards // 2)

    mine, rows_full, cot_near, cot_behind, cot_far = tied(
        mine, rows_full, cot_near, cot_behind, cot_far
    )
    theirs = other_core(mine)

    normed, inverse, partial = kernel_call(
        norm_kernel,
        [((2, NZ, TOK_DEV, deep), BF), square, ((TOK_DEV, q_cols + 2 * k_cols), F32)],
        [rows_full, mine], "norm", 60,
    )
    block = (2, TOK_DEV + EXTRA, deep)
    *attn_cuts, grad_value, terms = kernel_call(
        functools.partial(layer_kernel, q_heads),
        [cut] * 4 + [((TOK_DEV, k_cols), BF), ((peers,) + block, BF)],
        [normed, cosine, sine, allowed, home, cot_near, cot_behind, cot_far, mine, inverse, partial, theirs],
        "layer", 60, 0,
        [pltpu.VMEM((TOK_DEV, q_cols + 2 * k_cols), BF)],
    )
    total = lax.psum_scatter(terms, "tensor", scatter_dimension=0, tiled=False)
    (grad_hidden,) = kernel_call(
        finish_kernel, [((TOK_DEV, width), BF)],
        [hidden, gain[None, :], inverse, total], "finish", 60,
    )

    share = ((NZ * NX, rows_each, k_cols), BF)
    kept, given = kernel_call(value_kernel, [share, share], [normed, grad_value], "value", 60)
    pair = (kept.astype(F32) + other_core(given).astype(F32)).astype(BF)
    parts = lax.all_to_all(pair, ("z", "x"), split_axis=0, concat_axis=0, tiled=True)
    grad_value_weight = jnp.sum(parts.astype(F32), 0)

    attn_sent = [passed_along(attn_cuts[n], s) for n, s in enumerate(strides)]
    (attn_out,) = kernel_call(
        lay_kernel, [((CAP, q_cols), BF)], [dest, *attn_sent], "lay", 8
    )
    return (attn_out, grad_hidden, grad_value_weight)


def solution(mesh):
    fine = Mesh(mesh.devices.reshape(NZ, NX, NC, -1), DP + ("tensor",))
    both = P(DP, "tensor")
    return jax.shard_map(
        on_device,
        mesh=fine,
        in_specs=(both, P("tensor")) + (both,) * 4 + (P(),) * 4,
        out_specs=(both,) * 3,
        check_vma=False,
    )
```

```python
import functools

import jax
import jax.numpy as jnp
import numpy as np
from jax import lax
from jax.experimental import pallas as pl
from jax.experimental.pallas import tpu as pltpu
from jax.sharding import Mesh, PartitionSpec as P

D = 4096
HEAD = 128
TOK_DEV = 128
MAXLEN = 64
CAP = 256
SLOTS = 4
EXTRA = 16
EPSILON = 1e-05
ROPE_BASE = 500000.0
NZ, NX, NC = 8, 4, 2
DP = ("z", "x", "core")
BF = jnp.bfloat16
F32 = jnp.float32
MIB = 1024 * 1024


def moved(value, where):
    pairs = []
    for z in range(NZ):
        for x in range(NX):
            for c in range(NC):
                tz, tx, tc = where(z, x, c)
                pairs.append(((z * NX + x) * NC + c, ((tz % NZ) * NX + tx % NX) * NC + tc))
    return lax.ppermute(value, DP, pairs)


def other_core(value):
    return moved(value, lambda z, x, c: (z, x, 1 - c))


def passed_along(value, by):
    size = NZ * NX * NC
    return lax.ppermute(value, DP, [(i, (i + by) % size) for i in range(size)])


def tied(*values):
    return lax.optimization_barrier(values)


def dot_nn(a, b):
    return lax.dot_general(a, b, (((1,), (0,)), ((), ())), preferred_element_type=F32)


def dot_nt(a, b):
    return lax.dot_general(a, b, (((1,), (1,)), ((), ())), preferred_element_type=F32)


def dot_tn(a, b):
    return lax.dot_general(a, b, (((0,), (0,)), ((), ())), preferred_element_type=F32)


def place():
    z, x, c = [lax.axis_index(axis) for axis in DP]
    return (z * NX + x) * NC + c, z, x, c


def feature_order(width):
    natural = lax.broadcasted_iota(jnp.int32, (width, width), 0)
    place_in = lax.broadcasted_iota(jnp.int32, (width, width), 1)
    core = place_in >> 8
    x = (place_in >> 6) & (NX - 1)
    return jnp.where(natural == x * (NC * 64) + core * 64 + (place_in & 63), 1.0, 0.0).astype(BF)


def plan_kernel(
    strides, shards, get, put, send, smem, extra,
):
    len_ref, off_ref, shard_ref, start_ref = smem
    home_ref, dest_ref, cos_ref, sin_ref, allowed_ref, packed_ref = [put(3 + i) for i in range(6)]
    order = feature_order(packed_ref.shape[2] * packed_ref.shape[0])
    deep = packed_ref.shape[2]
    features = dot_nn(get(2)[...], order).astype(BF)
    gains = dot_nn(jnp.broadcast_to(get(3)[...], (EXTRA, 2 * deep)), order).astype(BF)
    for h in range(2):
        packed_ref[h, :TOK_DEV, :] = features[:, h * deep : (h + 1) * deep]
        packed_ref[h, TOK_DEV:, :] = gains[:, h * deep : (h + 1) * deep]
    send(8)
    me = place()[0]
    rows = lax.broadcasted_iota(jnp.int32, (TOK_DEV, TOK_DEV), 0)
    cols = lax.broadcasted_iota(jnp.int32, (TOK_DEV, TOK_DEV), 1)
    row_seq, row_pos = jnp.zeros_like(rows), jnp.zeros_like(rows)
    col_seq, col_pos = jnp.zeros_like(rows), jnp.zeros_like(rows)
    for e, stride in enumerate(strides):
        target = lax.rem(me + stride + shards, shards)
        source = lax.rem(me - stride + shards, shards)
        length = jnp.int32(0)
        offset = jnp.int32(0)
        in_len = jnp.int32(0)
        in_start = jnp.int32(0)
        for c in range(SLOTS):
            mine = shard_ref[c, me] == target
            length = length + jnp.where(mine, len_ref[c, me], 0)
            offset = offset + jnp.where(mine, off_ref[c, me], 0)
            theirs = shard_ref[c, source] == me
            in_len = in_len + jnp.where(theirs, len_ref[c, source], 0)
            in_start = in_start + jnp.where(theirs, start_ref[c, source], 0)
        inside = (rows >= offset) & (rows < offset + length)
        row_seq = jnp.where(inside, e, row_seq)
        row_pos = jnp.where(inside, rows - offset, row_pos)
        inside = (cols >= offset) & (cols < offset + length)
        col_seq = jnp.where(inside, e, col_seq)
        col_pos = jnp.where(inside, cols - offset, col_pos)
        at = slice(e * MAXLEN, (e + 1) * MAXLEN)
        t = lax.broadcasted_iota(jnp.int32, (MAXLEN, TOK_DEV), 0)
        r = lax.broadcasted_iota(jnp.int32, (MAXLEN, TOK_DEV), 1)
        home_ref[at, :] = jnp.where((r == t + offset) & (t < length), 1.0, 0.0).astype(BF)
        t = lax.broadcasted_iota(jnp.int32, (MAXLEN, CAP), 0)
        r = lax.broadcasted_iota(jnp.int32, (MAXLEN, CAP), 1)
        dest = jnp.where((r == t + in_start) & (t < in_len), 1.0, 0.0).astype(BF)
        dest_ref[at, :] = dest
        ref, lo = ((1, 0), (0, 0), (2, 0), (0, MAXLEN))[e]
        put(ref)[lo : lo + MAXLEN, :] = dot_nn(dest, get(1)[...]).astype(BF)
    allowed_ref[...] = jnp.where((row_seq == col_seq) & (col_pos <= row_pos), 1.0, 0.0)
    angles = row_pos.astype(F32) * get(0)[...]
    cos_ref[...] = jnp.cos(angles)
    sine = jnp.sin(angles)
    sin_ref[...] = jnp.where(cols < HEAD // 2, -sine, sine)


def norm_kernel(get, put, send, smem, extra):
    c = place()[3]
    rows_ref, normed_ref, inverse_ref, partial_ref = get(0), put(0), put(1), put(2)
    deep = rows_ref.shape[3]
    squares = jnp.zeros((TOK_DEV, 1), F32)
    for j in range(NZ):
        for h in range(2):
            part = rows_ref[j, h, :TOK_DEV, :].astype(F32)
            squares = squares + jnp.sum(part * part, 1, keepdims=True)
    inverse = lax.rsqrt(squares / D + EPSILON)
    inverse_ref[...] = jnp.broadcast_to(inverse, inverse_ref.shape)
    for n, half in enumerate((c, 1 - c)):
        for j in range(NZ):
            gain = rows_ref[j, half, TOK_DEV:, :].astype(F32)[0:1, :]
            part = rows_ref[j, half, :TOK_DEV, :].astype(F32) * inverse * gain
            normed_ref[n, j] = part.astype(BF)
    send(0)
    partial = jnp.zeros(partial_ref.shape, F32)
    for j in range(NZ):
        partial = partial + dot_nn(normed_ref[0, j], get(1)[j * deep : (j + 1) * deep, :])
    partial_ref[...] = partial


def value_kernel(get, put, send, smem, extra):
    kept_ref, given_ref = put(0), put(1)
    grad_value = get(1)[...]
    for n, ref in enumerate((kept_ref, given_ref)):
        for j in range(NZ):
            found = dot_tn(get(0)[n, j], grad_value).astype(BF)
            for x in range(NX):
                ref[j * NX + x] = found[x * 64 : (x + 1) * 64, :]


def layer_kernel(q_heads, get, put, send, smem, extra):
    (grads_ref,) = extra
    value_out_ref, terms_ref = put(4), put(5)
    c = place()[3]
    kv_at = q_heads * HEAD
    inverse = get(9)[:, 0:1]
    normed_ref = get(0)
    deep = normed_ref.shape[3]
    projected = get(10)[...]
    for j in range(NZ):
        projected = projected + dot_nn(normed_ref[1, j], get(11)[j * deep : (j + 1) * deep, :])
    cosine = get(1)[...]
    sine = get(2)[...]
    factor = HEAD ** (-0.5)
    home = get(4)[...]
    cot = jnp.concatenate(
        [get(6)[...], get(5)[:MAXLEN, :], get(7)[...]], 0
    )
    cot = dot_tn(home, cot).astype(BF)
    key_raw = projected[:, kv_at : kv_at + HEAD]
    value_raw = projected[:, kv_at + HEAD :]
    key = (key_raw * cosine + pltpu.roll(key_raw, HEAD // 2, 1) * sine).astype(BF)
    value = value_raw.astype(BF)
    heads = [slice(g * HEAD, (g + 1) * HEAD) for g in range(q_heads)]
    piles = [slice(g * TOK_DEV, (g + 1) * TOK_DEV) for g in range(q_heads)]
    cosines = jnp.concatenate([cosine] * q_heads, 0)
    sines = jnp.concatenate([sine] * q_heads, 0)
    query_raw = jnp.concatenate([projected[:, at] for at in heads], 0)
    query = (query_raw * cosines + pltpu.roll(query_raw, HEAD // 2, 1) * sines).astype(BF)
    grad_out = jnp.concatenate([cot[:, at] for at in heads], 0)
    scores = dot_nt(query, key) * factor
    scores = jnp.where(jnp.concatenate([get(3)[...]] * q_heads, 0) > 0.5, scores, F32(-1e30))
    exp_terms = jnp.exp(scores - jnp.max(scores, -1, keepdims=True))
    probs = exp_terms / jnp.sum(exp_terms, -1, keepdims=True)
    probs_low = probs.astype(BF)
    grad_probs = dot_nt(grad_out, value)
    mixed = dot_nn(probs_low, value).astype(BF)
    mixed = dot_nn(home, jnp.concatenate([mixed[at, :] for at in piles], 1)).astype(BF)
    for e in range(SLOTS):
        put(e)[...] = mixed[e * MAXLEN : (e + 1) * MAXLEN, :]
    grad_value = dot_tn(probs_low, grad_out)
    centre = jnp.sum(grad_probs * probs, -1, keepdims=True)
    grad_scores = (probs * (grad_probs - centre) * factor).astype(BF)
    grad_query = dot_nn(grad_scores, key)
    grad_key = dot_tn(grad_scores, query)
    grad_query = (grad_query * cosines - pltpu.roll(grad_query, HEAD // 2, 1) * sines).astype(BF)
    pile_dots = grad_query.astype(F32) * query_raw
    dots = jnp.zeros((TOK_DEV, HEAD), F32)
    for at, pile in zip(heads, piles):
        grads_ref[:, at] = grad_query[pile, :]
        dots = dots + pile_dots[pile, :]
    grad_key = (grad_key * cosine - pltpu.roll(grad_key, HEAD // 2, 1) * sine).astype(BF)
    grad_value = grad_value.astype(BF)
    grads_ref[:, kv_at : kv_at + HEAD] = grad_key
    grads_ref[:, kv_at + HEAD :] = grad_value
    value_out_ref[...] = grad_value
    dots = dots + grad_key.astype(F32) * key_raw + grad_value.astype(F32) * value_raw
    for e in range(SLOTS):
        send(e)
    share = jnp.sum(dots, 1, keepdims=True) / inverse
    share = jnp.transpose(jnp.broadcast_to(share, (TOK_DEV, TOK_DEV)))[0:EXTRA, :]
    high = share.astype(BF)
    low = (share - high.astype(F32)).astype(BF)
    tail = jnp.concatenate([high, low], 1)
    grads = grads_ref[...]
    for half, ref in ((c, 8), (1 - c, 11)):
        for j in range(NZ):
            found = dot_nt(grads, get(ref)[j * deep : (j + 1) * deep, :])
            terms_ref[j, half, :TOK_DEV, :] = found.astype(BF)
            terms_ref[j, half, TOK_DEV:, :] = tail


def finish_kernel(get, put, send, smem, extra):
    packed_ref, inverse, total_ref = get(0), get(1)[:, 0:1], get(2)
    share = total_ref[0, TOK_DEV:, :].astype(F32)
    share = share[0:1, :TOK_DEV] + share[0:1, TOK_DEV : 2 * TOK_DEV]
    row_dot = jnp.transpose(jnp.broadcast_to(share, (TOK_DEV, TOK_DEV)))[:, 0:1]
    row_dot = inverse * inverse * inverse * row_dot / D
    halves = []
    for h in range(2):
        gain = packed_ref[h, TOK_DEV:, :].astype(F32)[0:1, :]
        weighted = total_ref[h, :TOK_DEV, :].astype(F32) * gain
        here = packed_ref[h, :TOK_DEV, :].astype(F32)
        halves.append((inverse * weighted - here * row_dot).astype(BF))
    grad = jnp.concatenate(halves, 1)
    put(0)[...] = dot_nt(grad, feature_order(grad.shape[1])).astype(BF)


def lay_kernel(get, put, send, smem, extra):
    rows = jnp.concatenate(
        [get(1 + e)[...] for e in range(SLOTS)], 0
    )
    put(0)[...] = dot_tn(get(0)[...], rows).astype(BF)


def kernel_call(body, outs, args, name, mib, scalars=0, scratch=()):
    shapes = [jax.ShapeDtypeStruct(s, d) for s, d in outs]
    arrays = args[scalars:]
    n_in, n_out = len(arrays), len(shapes)

    def kernel(*refs):
        smem, refs = refs[:scalars], refs[scalars:]
        ins, refs = refs[:n_in], refs[n_in:]
        out, refs = refs[:n_out], refs[n_out:]
        in_buf, refs = refs[:n_in], refs[n_in:]
        out_buf, refs = refs[:n_out], refs[n_out:]
        in_sem, out_sem, extra = refs[0], refs[1], refs[2:]
        loads = [pltpu.make_async_copy(ins[i], in_buf[i], in_sem.at[i]) for i in range(n_in)]
        stores = [pltpu.make_async_copy(out_buf[i], out[i], out_sem.at[i]) for i in range(n_out)]
        for load in loads:
            load.start()
        waited, sent = set(), set()

        def get(i):
            if i not in waited:
                waited.add(i)
                loads[i].wait()
            return in_buf[i]

        def send(i):
            if i not in sent:
                sent.add(i)
                stores[i].start()

        body(get, lambda i: out_buf[i], send, smem, extra)
        for i in range(n_in):
            get(i)
        for i in range(n_out):
            send(i)
        for store in stores:
            store.wait()

    hbm = pl.BlockSpec(memory_space=pltpu.HBM)
    return pl.pallas_call(
        kernel,
        out_shape=shapes,
        in_specs=[pl.BlockSpec(memory_space=pltpu.SMEM)] * scalars + [hbm] * n_in,
        out_specs=[hbm] * n_out,
        scratch_shapes=[pltpu.VMEM(v.shape, v.dtype) for v in arrays]
        + [pltpu.VMEM(v.shape, v.dtype) for v in shapes]
        + [pltpu.SemaphoreType.DMA((n_in,)), pltpu.SemaphoreType.DMA((n_out,))]
        + list(scratch),
        compiler_params=pltpu.CompilerParams(vmem_limit_bytes=mib * MIB),
        name=name,
    )(*args)


def on_device(
    hidden, gain, w_query, w_key, w_value, cotangent, seq_length, home_offset, dest_shard, dest_offset
):
    shards = NZ * NX * NC
    peers = lax.axis_size("tensor")
    me, z, x, c = place()
    strides = [-1, 1, shards // 2, shards // 2 + 1]
    width = hidden.shape[1]
    deep = width // 2
    q_cols = w_query.shape[1]
    k_cols = w_key.shape[1]
    q_heads = q_cols // HEAD
    rows_each = D // shards

    own = jnp.concatenate([w_query, w_key, w_value], 1)
    own_half = lax.all_gather(own, "x", axis=0, tiled=True)
    own_half, cotangent = tied(own_half, cotangent)
    mine = lax.all_gather(own_half, "z", axis=0, tiled=True)

    half = HEAD // 2
    freq = np.power(np.float32(ROPE_BASE), -(np.arange(half, dtype=np.float32) * np.float32(2.0 / HEAD)))
    freq = jnp.asarray(np.concatenate([freq, freq])[None, :].astype(np.float32))
    square = ((TOK_DEV, TOK_DEV), F32)
    cut = ((MAXLEN, q_cols), BF)
    wide = ((2 * MAXLEN, q_cols), BF)
    cot_near, cot_behind, cot_far, home, dest, cosine, sine, allowed, packed = kernel_call(
        functools.partial(plan_kernel, strides, shards),
        [wide, cut, cut] + [((SLOTS * MAXLEN, TOK_DEV), BF), ((SLOTS * MAXLEN, CAP), BF)] + [square] * 3
        + [((2, TOK_DEV + EXTRA, deep), BF)],
        [seq_length.T, home_offset.T, dest_shard.T, dest_offset.T, freq, cotangent, hidden, gain[None, :]],
        "plan", 60, 4,
    )
    copies = jnp.broadcast_to(packed[None], (peers,) + packed.shape)
    rows_full = lax.all_to_all(copies, "tensor", split_axis=0, concat_axis=0, tiled=True)
    cot_near = passed_along(cot_near, -1)
    cot_behind = passed_along(cot_behind, 1)
    cot_far = passed_along(jnp.concatenate([cot_far, cot_near[MAXLEN:]], 0), shards // 2)

    mine, rows_full, cot_near, cot_behind, cot_far = tied(
        mine, rows_full, cot_near, cot_behind, cot_far
    )
    theirs = other_core(mine)

    normed, inverse, partial = kernel_call(
        norm_kernel,
        [((2, NZ, TOK_DEV, deep), BF), square, ((TOK_DEV, q_cols + 2 * k_cols), F32)],
        [rows_full, mine], "norm", 60,
    )
    block = (2, TOK_DEV + EXTRA, deep)
    *attn_cuts, grad_value, terms = kernel_call(
        functools.partial(layer_kernel, q_heads),
        [cut] * 4 + [((TOK_DEV, k_cols), BF), ((peers,) + block, BF)],
        [normed, cosine, sine, allowed, home, cot_near, cot_behind, cot_far, mine, inverse, partial, theirs],
        "layer", 60, 0,
        [pltpu.VMEM((TOK_DEV, q_cols + 2 * k_cols), BF)],
    )
    total = lax.psum_scatter(terms, "tensor", scatter_dimension=0, tiled=False)
    (grad_hidden,) = kernel_call(
        finish_kernel, [((TOK_DEV, width), BF)],
        [packed, inverse, total], "finish", 60,
    )

    share = ((NZ * NX, rows_each, k_cols), BF)
    kept, given = kernel_call(value_kernel, [share, share], [normed, grad_value], "value", 60)
    pair = (kept.astype(F32) + other_core(given).astype(F32)).astype(BF)
    parts = lax.all_to_all(pair, ("z", "x"), split_axis=0, concat_axis=0, tiled=True)
    grad_value_weight = jnp.sum(parts.astype(F32), 0)

    attn_sent = [passed_along(attn_cuts[n], s) for n, s in enumerate(strides)]
    (attn_out,) = kernel_call(
        lay_kernel, [((CAP, q_cols), BF)], [dest, *attn_sent], "lay", 8
    )
    return (attn_out, grad_hidden, grad_value_weight)


def solution(mesh):
    fine = Mesh(mesh.devices.reshape(NZ, NX, NC, -1), DP + ("tensor",))
    both = P(DP, "tensor")
    return jax.shard_map(
        on_device,
        mesh=fine,
        in_specs=(both, P("tensor")) + (both,) * 4 + (P(),) * 4,
        out_specs=(both,) * 3,
        check_vma=False,
    )
```

```python
import functools

import jax
import jax.numpy as jnp
import numpy as np
from jax import lax
from jax.experimental import pallas as pl
from jax.experimental.pallas import tpu as pltpu
from jax.sharding import Mesh, PartitionSpec as P

D = 4096
HEAD = 128
TOK_DEV = 128
MAXLEN = 64
CAP = 256
SLOTS = 4
EXTRA = 16
EPSILON = 1e-05
ROPE_BASE = 500000.0
NZ, NX, NC = 8, 4, 2
DP = ("z", "x", "core")
BF = jnp.bfloat16
F32 = jnp.float32
MIB = 1024 * 1024


def moved(value, where):
    pairs = []
    for z in range(NZ):
        for x in range(NX):
            for c in range(NC):
                tz, tx, tc = where(z, x, c)
                pairs.append(((z * NX + x) * NC + c, ((tz % NZ) * NX + tx % NX) * NC + tc))
    return lax.ppermute(value, DP, pairs)


def other_core(value):
    return moved(value, lambda z, x, c: (z, x, 1 - c))


def passed_along(value, by):
    size = NZ * NX * NC
    return lax.ppermute(value, DP, [(i, (i + by) % size) for i in range(size)])


def tied(*values):
    return lax.optimization_barrier(values)


def dot_nn(a, b):
    return lax.dot_general(a, b, (((1,), (0,)), ((), ())), preferred_element_type=F32)


def dot_nt(a, b):
    return lax.dot_general(a, b, (((1,), (1,)), ((), ())), preferred_element_type=F32)


def dot_tn(a, b):
    return lax.dot_general(a, b, (((0,), (0,)), ((), ())), preferred_element_type=F32)


def place():
    z, x, c = [lax.axis_index(axis) for axis in DP]
    return (z * NX + x) * NC + c, z, x, c


def feature_order(width):
    natural = lax.broadcasted_iota(jnp.int32, (width, width), 0)
    place_in = lax.broadcasted_iota(jnp.int32, (width, width), 1)
    core = place_in >> 8
    x = (place_in >> 6) & (NX - 1)
    return jnp.where(natural == x * (NC * 64) + core * 64 + (place_in & 63), 1.0, 0.0).astype(BF)


def plan_kernel(
    strides, shards, get, put, send, smem, extra,
):
    len_ref, off_ref, shard_ref, start_ref = smem
    home_ref, dest_ref, cos_ref, sin_ref, allowed_ref, packed_ref = [put(3 + i) for i in range(6)]
    deep = packed_ref.shape[1]
    order = feature_order(2 * deep)
    features = dot_nn(get(2)[...], order).astype(BF)
    gains = dot_nn(jnp.broadcast_to(get(3)[...], (EXTRA, 2 * deep)), order)
    for h in range(2):
        packed_ref[h * TOK_DEV : (h + 1) * TOK_DEV, :] = features[:, h * deep : (h + 1) * deep]
    gains = jnp.concatenate(
        [gains[: EXTRA // 2, :deep], gains[: EXTRA // 2, deep:]], 0
    )
    packed_ref[2 * TOK_DEV :, :] = gains.astype(BF)
    send(8)
    put(9)[...] = order
    send(9)
    me = place()[0]
    rows = lax.broadcasted_iota(jnp.int32, (TOK_DEV, TOK_DEV), 0)
    cols = lax.broadcasted_iota(jnp.int32, (TOK_DEV, TOK_DEV), 1)
    row_seq, row_pos = jnp.zeros_like(rows), jnp.zeros_like(rows)
    col_seq, col_pos = jnp.zeros_like(rows), jnp.zeros_like(rows)
    for e, stride in enumerate(strides):
        target = lax.rem(me + stride + shards, shards)
        source = lax.rem(me - stride + shards, shards)
        length = jnp.int32(0)
        offset = jnp.int32(0)
        in_len = jnp.int32(0)
        in_start = jnp.int32(0)
        for c in range(SLOTS):
            mine = shard_ref[c, me] == target
            length = length + jnp.where(mine, len_ref[c, me], 0)
            offset = offset + jnp.where(mine, off_ref[c, me], 0)
            theirs = shard_ref[c, source] == me
            in_len = in_len + jnp.where(theirs, len_ref[c, source], 0)
            in_start = in_start + jnp.where(theirs, start_ref[c, source], 0)
        inside = (rows >= offset) & (rows < offset + length)
        row_seq = jnp.where(inside, e, row_seq)
        row_pos = jnp.where(inside, rows - offset, row_pos)
        inside = (cols >= offset) & (cols < offset + length)
        col_seq = jnp.where(inside, e, col_seq)
        col_pos = jnp.where(inside, cols - offset, col_pos)
        at = slice(e * MAXLEN, (e + 1) * MAXLEN)
        t = lax.broadcasted_iota(jnp.int32, (MAXLEN, TOK_DEV), 0)
        r = lax.broadcasted_iota(jnp.int32, (MAXLEN, TOK_DEV), 1)
        home_ref[at, :] = jnp.where((r == t + offset) & (t < length), 1.0, 0.0).astype(BF)
        t = lax.broadcasted_iota(jnp.int32, (MAXLEN, CAP), 0)
        r = lax.broadcasted_iota(jnp.int32, (MAXLEN, CAP), 1)
        dest = jnp.where((r == t + in_start) & (t < in_len), 1.0, 0.0).astype(BF)
        dest_ref[at, :] = dest
        ref, lo = ((1, 0), (0, 0), (2, 0), (0, MAXLEN))[e]
        put(ref)[lo : lo + MAXLEN, :] = dot_nn(dest, get(1)[...]).astype(BF)
    allowed_ref[...] = jnp.where((row_seq == col_seq) & (col_pos <= row_pos), 1.0, 0.0)
    angles = row_pos.astype(F32) * get(0)[...]
    cos_ref[...] = jnp.cos(angles)
    sine = jnp.sin(angles)
    sin_ref[...] = jnp.where(cols < HEAD // 2, -sine, sine)


def norm_kernel(get, put, send, smem, extra):
    c = place()[3]
    rows_ref, normed_ref, inverse_ref, partial_ref = get(0), put(0), put(1), put(2)
    deep = rows_ref.shape[2]
    squares = jnp.zeros((TOK_DEV, 1), F32)
    for j in range(NZ):
        for h in range(2):
            part = rows_ref[j, h * TOK_DEV : (h + 1) * TOK_DEV, :].astype(F32)
            squares = squares + jnp.sum(part * part, 1, keepdims=True)
    inverse = lax.rsqrt(squares / D + EPSILON)
    inverse_ref[...] = jnp.broadcast_to(inverse, inverse_ref.shape)
    for n, half in enumerate((c, 1 - c)):
        for j in range(NZ):
            gains = rows_ref[j, 2 * TOK_DEV :, :].astype(F32)
            gain = jnp.where(half == 0, gains[0:1, :], gains[EXTRA // 2 : EXTRA // 2 + 1, :])
            at = pl.ds(pl.multiple_of(half * TOK_DEV, TOK_DEV), TOK_DEV)
            part = rows_ref[j, at, :].astype(F32) * inverse * gain
            normed_ref[n, :, j * deep : (j + 1) * deep] = part.astype(BF)
    send(0)
    partial_ref[...] = dot_nn(normed_ref[0], get(1)[...])


def value_kernel(get, put, send, smem, extra):
    kept_ref, given_ref = put(0), put(1)
    grad_value = get(1)[...]
    for n, ref in enumerate((kept_ref, given_ref)):
        for j in range(NZ):
            found = dot_tn(get(0)[n, :, j * 256 : (j + 1) * 256], grad_value).astype(BF)
            for x in range(NX):
                ref[j * NX + x] = found[x * 64 : (x + 1) * 64, :]


def layer_kernel(q_heads, get, put, send, smem, extra):
    (grads_ref,) = extra
    value_out_ref, terms_ref = put(4), put(5)
    c = place()[3]
    kv_at = q_heads * HEAD
    inverse = get(9)[:, 0:1]
    deep = terms_ref.shape[2]
    projected = get(10)[...] + dot_nn(get(0)[1], get(8)[...])
    cosine = get(1)[...]
    sine = get(2)[...]
    factor = HEAD ** (-0.5)
    home = get(4)[...]
    cot = jnp.concatenate(
        [get(6)[...], get(5)[:MAXLEN, :], get(7)[...]], 0
    )
    cot = dot_tn(home, cot).astype(BF)
    key_raw = projected[:, kv_at : kv_at + HEAD]
    value_raw = projected[:, kv_at + HEAD :]
    key = (key_raw * cosine + pltpu.roll(key_raw, HEAD // 2, 1) * sine).astype(BF)
    value = value_raw.astype(BF)
    heads = [slice(g * HEAD, (g + 1) * HEAD) for g in range(q_heads)]
    piles = [slice(g * TOK_DEV, (g + 1) * TOK_DEV) for g in range(q_heads)]
    cosines = jnp.concatenate([cosine] * q_heads, 0)
    sines = jnp.concatenate([sine] * q_heads, 0)
    query_raw = jnp.concatenate([projected[:, at] for at in heads], 0)
    query = (query_raw * cosines + pltpu.roll(query_raw, HEAD // 2, 1) * sines).astype(BF)
    grad_out = jnp.concatenate([cot[:, at] for at in heads], 0)
    scores = dot_nt(query, key) * factor
    scores = jnp.where(jnp.concatenate([get(3)[...]] * q_heads, 0) > 0.5, scores, F32(-1e30))
    exp_terms = jnp.exp(scores - jnp.max(scores, -1, keepdims=True))
    probs = exp_terms / jnp.sum(exp_terms, -1, keepdims=True)
    probs_low = probs.astype(BF)
    grad_probs = dot_nt(grad_out, value)
    mixed = dot_nn(probs_low, value).astype(BF)
    mixed = dot_nn(home, jnp.concatenate([mixed[at, :] for at in piles], 1)).astype(BF)
    for e in range(SLOTS):
        put(e)[...] = mixed[e * MAXLEN : (e + 1) * MAXLEN, :]
    grad_value = dot_tn(probs_low, grad_out)
    centre = jnp.sum(grad_probs * probs, -1, keepdims=True)
    grad_scores = (probs * (grad_probs - centre) * factor).astype(BF)
    grad_query = dot_nn(grad_scores, key)
    grad_key = dot_tn(grad_scores, query)
    grad_query = (grad_query * cosines - pltpu.roll(grad_query, HEAD // 2, 1) * sines).astype(BF)
    pile_dots = grad_query.astype(F32) * query_raw
    dots = jnp.zeros((TOK_DEV, HEAD), F32)
    for at, pile in zip(heads, piles):
        grads_ref[:, at] = grad_query[pile, :]
        dots = dots + pile_dots[pile, :]
    grad_key = (grad_key * cosine - pltpu.roll(grad_key, HEAD // 2, 1) * sine).astype(BF)
    grad_value = grad_value.astype(BF)
    grads_ref[:, kv_at : kv_at + HEAD] = grad_key
    grads_ref[:, kv_at + HEAD :] = grad_value
    value_out_ref[...] = grad_value
    dots = dots + grad_key.astype(F32) * key_raw + grad_value.astype(F32) * value_raw
    for e in range(SLOTS):
        send(e)
    share = jnp.sum(dots, 1, keepdims=True) / inverse
    share = jnp.transpose(jnp.broadcast_to(share, (TOK_DEV, TOK_DEV)))[0:EXTRA, :]
    high = share.astype(BF)
    low = (share - high.astype(F32)).astype(BF)
    tail = jnp.concatenate([high, low], 1)
    grads = grads_ref[...]
    for half, ref in ((1 - c, 8), (c, 11)):
        for j in range(NZ):
            found = dot_nt(grads, get(ref)[j * deep : (j + 1) * deep, :])
            terms_ref[j, pl.ds(pl.multiple_of(half * TOK_DEV, TOK_DEV), TOK_DEV), :] = found.astype(BF)
    for j in range(NZ):
        terms_ref[j, 2 * TOK_DEV :, :] = tail


def finish_kernel(get, put, send, smem, extra):
    packed_ref, inverse, total_ref = get(0), get(1)[:, 0:1], get(2)
    share = total_ref[2 * TOK_DEV :, :].astype(F32)
    share = share[0:1, :TOK_DEV] + share[0:1, TOK_DEV : 2 * TOK_DEV]
    row_dot = jnp.transpose(jnp.broadcast_to(share, (TOK_DEV, TOK_DEV)))[:, 0:1]
    row_dot = inverse * inverse * inverse * row_dot / D
    halves = []
    for h in range(2):
        gain = packed_ref[2 * TOK_DEV :, :].astype(F32)[h * (EXTRA // 2) : h * (EXTRA // 2) + 1, :]
        rows = slice(h * TOK_DEV, (h + 1) * TOK_DEV)
        weighted = total_ref[rows, :].astype(F32) * gain
        here = packed_ref[rows, :].astype(F32)
        halves.append((inverse * weighted - here * row_dot).astype(BF))
    grad = jnp.concatenate(halves, 1)
    put(0)[...] = dot_nt(grad, get(3)[...]).astype(BF)


def lay_kernel(get, put, send, smem, extra):
    rows = jnp.concatenate(
        [get(1 + e)[...] for e in range(SLOTS)], 0
    )
    put(0)[...] = dot_tn(get(0)[...], rows).astype(BF)


def kernel_call(body, outs, args, name, mib, scalars=0, scratch=()):
    shapes = [jax.ShapeDtypeStruct(s, d) for s, d in outs]
    arrays = args[scalars:]
    n_in, n_out = len(arrays), len(shapes)

    def kernel(*refs):
        smem, refs = refs[:scalars], refs[scalars:]
        ins, refs = refs[:n_in], refs[n_in:]
        out, refs = refs[:n_out], refs[n_out:]
        in_buf, refs = refs[:n_in], refs[n_in:]
        out_buf, refs = refs[:n_out], refs[n_out:]
        in_sem, out_sem, extra = refs[0], refs[1], refs[2:]
        loads = [pltpu.make_async_copy(ins[i], in_buf[i], in_sem.at[i]) for i in range(n_in)]
        stores = [pltpu.make_async_copy(out_buf[i], out[i], out_sem.at[i]) for i in range(n_out)]
        for load in loads:
            load.start()
        waited, sent = set(), set()

        def get(i):
            if i not in waited:
                waited.add(i)
                loads[i].wait()
            return in_buf[i]

        def send(i):
            if i not in sent:
                sent.add(i)
                stores[i].start()

        body(get, lambda i: out_buf[i], send, smem, extra)
        for i in range(n_in):
            get(i)
        for i in range(n_out):
            send(i)
        for store in stores:
            store.wait()

    hbm = pl.BlockSpec(memory_space=pltpu.HBM)
    return pl.pallas_call(
        kernel,
        out_shape=shapes,
        in_specs=[pl.BlockSpec(memory_space=pltpu.SMEM)] * scalars + [hbm] * n_in,
        out_specs=[hbm] * n_out,
        scratch_shapes=[pltpu.VMEM(v.shape, v.dtype) for v in arrays]
        + [pltpu.VMEM(v.shape, v.dtype) for v in shapes]
        + [pltpu.SemaphoreType.DMA((n_in,)), pltpu.SemaphoreType.DMA((n_out,))]
        + list(scratch),
        compiler_params=pltpu.CompilerParams(vmem_limit_bytes=mib * MIB),
        name=name,
    )(*args)


def on_device(
    hidden, gain, w_query, w_key, w_value, cotangent, seq_length, home_offset, dest_shard, dest_offset
):
    shards = NZ * NX * NC
    peers = lax.axis_size("tensor")
    me, z, x, c = place()
    strides = [-1, 1, shards // 2, shards // 2 + 1]
    width = hidden.shape[1]
    deep = width // 2
    q_cols = w_query.shape[1]
    k_cols = w_key.shape[1]
    q_heads = q_cols // HEAD
    rows_each = D // shards

    own = jnp.concatenate([w_query, w_key, w_value], 1)
    own_half = lax.all_to_all(
        jnp.broadcast_to(own[None], (NX,) + own.shape), "x", split_axis=0, concat_axis=0, tiled=True
    ).reshape(NX * own.shape[0], own.shape[1])
    own_half, cotangent = tied(own_half, cotangent)
    mine = lax.all_gather(own_half, "z", axis=0, tiled=True)

    half = HEAD // 2
    freq = np.power(np.float32(ROPE_BASE), -(np.arange(half, dtype=np.float32) * np.float32(2.0 / HEAD)))
    freq = jnp.asarray(np.concatenate([freq, freq])[None, :].astype(np.float32))
    square = ((TOK_DEV, TOK_DEV), F32)
    block = (2 * TOK_DEV + EXTRA, deep)
    cut = ((MAXLEN, q_cols), BF)
    wide = ((2 * MAXLEN, q_cols), BF)
    cot_near, cot_behind, cot_far, home, dest, cosine, sine, allowed, packed, order = kernel_call(
        functools.partial(plan_kernel, strides, shards),
        [wide, cut, cut] + [((SLOTS * MAXLEN, TOK_DEV), BF), ((SLOTS * MAXLEN, CAP), BF)] + [square] * 3
        + [(block, BF), ((width, width), BF)],
        [seq_length.T, home_offset.T, dest_shard.T, dest_offset.T, freq, cotangent, hidden, gain[None, :]],
        "plan", 60, 4,
    )
    copies = jnp.broadcast_to(packed[None], (peers,) + packed.shape)
    rows_full = lax.all_to_all(copies, "tensor", split_axis=0, concat_axis=0, tiled=True)
    cot_near = passed_along(cot_near, -1)
    cot_behind = passed_along(cot_behind, 1)
    cot_far = passed_along(jnp.concatenate([cot_far, cot_near[MAXLEN:]], 0), shards // 2)

    mine, rows_full, cot_near, cot_behind, cot_far = tied(
        mine, rows_full, cot_near, cot_behind, cot_far
    )
    theirs = other_core(mine)

    normed, inverse, partial = kernel_call(
        norm_kernel,
        [((2, TOK_DEV, NZ * deep), BF), square, ((TOK_DEV, q_cols + 2 * k_cols), F32)],
        [rows_full, mine], "norm", 60,
    )
    *attn_cuts, grad_value, terms = kernel_call(
        functools.partial(layer_kernel, q_heads),
        [cut] * 4 + [((TOK_DEV, k_cols), BF), ((peers,) + block, BF)],
        [normed, cosine, sine, allowed, home, cot_near, cot_behind, cot_far, theirs, inverse, partial, mine],
        "layer", 60, 0,
        [pltpu.VMEM((TOK_DEV, q_cols + 2 * k_cols), BF)],
    )
    total = lax.psum_scatter(terms, "tensor", scatter_dimension=0, tiled=False)
    (grad_hidden,) = kernel_call(
        finish_kernel, [((TOK_DEV, width), BF)],
        [packed, inverse, total, order], "finish", 60,
    )

    share = ((NZ * NX, rows_each, k_cols), BF)
    kept, given = kernel_call(value_kernel, [share, share], [normed, grad_value], "value", 60)
    pair = (kept.astype(F32) + other_core(given).astype(F32)).astype(BF)
    parts = lax.all_to_all(pair, ("z", "x"), split_axis=0, concat_axis=0, tiled=True)
    grad_value_weight = jnp.sum(parts.astype(F32), 0)

    attn_sent = [passed_along(attn_cuts[n], s) for n, s in enumerate(strides)]
    (attn_out,) = kernel_call(
        lay_kernel, [((CAP, q_cols), BF)], [dest, *attn_sent], "lay", 8
    )
    return (attn_out, grad_hidden, grad_value_weight)


def solution(mesh):
    fine = Mesh(mesh.devices.reshape(NZ, NX, NC, -1), DP + ("tensor",))
    both = P(DP, "tensor")
    return jax.shard_map(
        on_device,
        mesh=fine,
        in_specs=(both, P("tensor")) + (both,) * 4 + (P(),) * 4,
        out_specs=(both,) * 3,
        check_vma=False,
    )
```

```python
import functools

import jax
import jax.numpy as jnp
import numpy as np
from jax import lax
from jax.experimental import pallas as pl
from jax.experimental.pallas import tpu as pltpu
from jax.sharding import Mesh, PartitionSpec as P

D = 4096
HEAD = 128
TOK_DEV = 128
MAXLEN = 64
CAP = 256
SLOTS = 4
EXTRA = 16
EPSILON = 1e-05
ROPE_BASE = 500000.0
NZ, NX, NC = 8, 4, 2
DP = ("z", "x", "core")
BF = jnp.bfloat16
F32 = jnp.float32
MIB = 1024 * 1024


def moved(value, where):
    pairs = []
    for z in range(NZ):
        for x in range(NX):
            for c in range(NC):
                tz, tx, tc = where(z, x, c)
                pairs.append(((z * NX + x) * NC + c, ((tz % NZ) * NX + tx % NX) * NC + tc))
    return lax.ppermute(value, DP, pairs)


def other_core(value):
    return moved(value, lambda z, x, c: (z, x, 1 - c))


def passed_along(value, by):
    size = NZ * NX * NC
    return lax.ppermute(value, DP, [(i, (i + by) % size) for i in range(size)])


def tied(*values):
    return lax.optimization_barrier(values)


def dot_nn(a, b):
    return lax.dot_general(a, b, (((1,), (0,)), ((), ())), preferred_element_type=F32)


def dot_nt(a, b):
    return lax.dot_general(a, b, (((1,), (1,)), ((), ())), preferred_element_type=F32)


def dot_tn(a, b):
    return lax.dot_general(a, b, (((0,), (0,)), ((), ())), preferred_element_type=F32)


def place():
    z, x, c = [lax.axis_index(axis) for axis in DP]
    return (z * NX + x) * NC + c, z, x, c


def feature_order(width):
    natural = lax.broadcasted_iota(jnp.int32, (width, width), 0)
    place_in = lax.broadcasted_iota(jnp.int32, (width, width), 1)
    core = place_in >> 8
    x = (place_in >> 6) & (NX - 1)
    return jnp.where(natural == x * (NC * 64) + core * 64 + (place_in & 63), 1.0, 0.0).astype(BF)


def plan_kernel(
    strides, shards, get, put, send, smem, extra,
):
    len_ref, off_ref, shard_ref, start_ref = smem
    home_ref, dest_ref, cos_ref, sin_ref, allowed_ref, packed_ref = [put(3 + i) for i in range(6)]
    deep = packed_ref.shape[1]
    order = feature_order(2 * deep)
    features = dot_nn(get(2)[...], order).astype(BF)
    gains = dot_nn(jnp.broadcast_to(get(3)[...], (EXTRA, 2 * deep)), order)
    for h in range(2):
        packed_ref[h * TOK_DEV : (h + 1) * TOK_DEV, :] = features[:, h * deep : (h + 1) * deep]
    gains = jnp.concatenate(
        [gains[: EXTRA // 2, :deep], gains[: EXTRA // 2, deep:]], 0
    )
    packed_ref[2 * TOK_DEV :, :] = gains.astype(BF)
    send(8)
    put(9)[...] = order
    send(9)
    me = place()[0]
    rows = lax.broadcasted_iota(jnp.int32, (TOK_DEV, TOK_DEV), 0)
    cols = lax.broadcasted_iota(jnp.int32, (TOK_DEV, TOK_DEV), 1)
    row_seq, row_pos = jnp.zeros_like(rows), jnp.zeros_like(rows)
    col_seq, col_pos = jnp.zeros_like(rows), jnp.zeros_like(rows)
    for e, stride in enumerate(strides):
        target = lax.rem(me + stride + shards, shards)
        source = lax.rem(me - stride + shards, shards)
        length = jnp.int32(0)
        offset = jnp.int32(0)
        in_len = jnp.int32(0)
        in_start = jnp.int32(0)
        for c in range(SLOTS):
            mine = shard_ref[c, me] == target
            length = length + jnp.where(mine, len_ref[c, me], 0)
            offset = offset + jnp.where(mine, off_ref[c, me], 0)
            theirs = shard_ref[c, source] == me
            in_len = in_len + jnp.where(theirs, len_ref[c, source], 0)
            in_start = in_start + jnp.where(theirs, start_ref[c, source], 0)
        inside = (rows >= offset) & (rows < offset + length)
        row_seq = jnp.where(inside, e, row_seq)
        row_pos = jnp.where(inside, rows - offset, row_pos)
        inside = (cols >= offset) & (cols < offset + length)
        col_seq = jnp.where(inside, e, col_seq)
        col_pos = jnp.where(inside, cols - offset, col_pos)
        at = slice(e * MAXLEN, (e + 1) * MAXLEN)
        t = lax.broadcasted_iota(jnp.int32, (MAXLEN, TOK_DEV), 0)
        r = lax.broadcasted_iota(jnp.int32, (MAXLEN, TOK_DEV), 1)
        home_ref[at, :] = jnp.where((r == t + offset) & (t < length), 1.0, 0.0).astype(BF)
        t = lax.broadcasted_iota(jnp.int32, (MAXLEN, CAP), 0)
        r = lax.broadcasted_iota(jnp.int32, (MAXLEN, CAP), 1)
        dest = jnp.where((r == t + in_start) & (t < in_len), 1.0, 0.0).astype(BF)
        dest_ref[at, :] = dest
        ref, lo = ((1, 0), (0, 0), (2, 0), (0, MAXLEN))[e]
        put(ref)[lo : lo + MAXLEN, :] = dot_nn(dest, get(1)[...]).astype(BF)
    allowed_ref[...] = jnp.where((row_seq == col_seq) & (col_pos <= row_pos), 1.0, 0.0)
    angles = row_pos.astype(F32) * get(0)[...]
    cos_ref[...] = jnp.cos(angles)
    sine = jnp.sin(angles)
    sin_ref[...] = jnp.where(cols < HEAD // 2, -sine, sine)


def norm_kernel(get, put, send, smem, extra):
    c = place()[3]
    rows_ref, normed_ref, inverse_ref, partial_ref = get(0), put(0), put(1), put(2)
    cot = jnp.concatenate([get(4)[...], get(3)[:MAXLEN, :], get(5)[...]], 0)
    cot = dot_tn(get(2)[...], cot).astype(BF)
    for g in range(cot.shape[1] // HEAD):
        put(3)[g * TOK_DEV : (g + 1) * TOK_DEV, :] = cot[:, g * HEAD : (g + 1) * HEAD]
    send(3)
    deep = rows_ref.shape[2]
    squares = jnp.zeros((TOK_DEV, 1), F32)
    for j in range(NZ):
        for h in range(2):
            part = rows_ref[j, h * TOK_DEV : (h + 1) * TOK_DEV, :].astype(F32)
            squares = squares + jnp.sum(part * part, 1, keepdims=True)
    inverse = lax.rsqrt(squares / D + EPSILON)
    inverse_ref[...] = jnp.broadcast_to(inverse, inverse_ref.shape)
    for n, half in enumerate((c, 1 - c)):
        for j in range(NZ):
            gains = rows_ref[j, 2 * TOK_DEV :, :].astype(F32)
            gain = jnp.where(half == 0, gains[0:1, :], gains[EXTRA // 2 : EXTRA // 2 + 1, :])
            at = pl.ds(pl.multiple_of(half * TOK_DEV, TOK_DEV), TOK_DEV)
            part = rows_ref[j, at, :].astype(F32) * inverse * gain
            normed_ref[n, :, j * deep : (j + 1) * deep] = part.astype(BF)
    send(0)
    partial_ref[...] = dot_nn(normed_ref[0], get(1)[...])


def value_kernel(get, put, send, smem, extra):
    kept_ref, given_ref = put(0), put(1)
    grad_value = get(1)[...]
    for n, ref in enumerate((kept_ref, given_ref)):
        for j in range(NZ):
            found = dot_tn(get(0)[n, :, j * 256 : (j + 1) * 256], grad_value).astype(BF)
            for x in range(NX):
                ref[j * NX + x] = found[x * 64 : (x + 1) * 64, :]


def layer_kernel(q_heads, get, put, send, smem, extra):
    (grads_ref,) = extra
    value_out_ref, terms_ref = put(4), put(5)
    c = place()[3]
    kv_at = q_heads * HEAD
    inverse = get(7)[:, 0:1]
    deep = terms_ref.shape[2]
    projected = get(8)[...] + dot_nn(get(0)[1], get(6)[...])
    cosine = get(1)[...]
    sine = get(2)[...]
    factor = HEAD ** (-0.5)
    home = get(4)[...]
    key_raw = projected[:, kv_at : kv_at + HEAD]
    value_raw = projected[:, kv_at + HEAD :]
    key = (key_raw * cosine + pltpu.roll(key_raw, HEAD // 2, 1) * sine).astype(BF)
    value = value_raw.astype(BF)
    heads = [slice(g * HEAD, (g + 1) * HEAD) for g in range(q_heads)]
    piles = [slice(g * TOK_DEV, (g + 1) * TOK_DEV) for g in range(q_heads)]
    cosines = jnp.concatenate([cosine] * q_heads, 0)
    sines = jnp.concatenate([sine] * q_heads, 0)
    query_raw = jnp.concatenate([projected[:, at] for at in heads], 0)
    query = (query_raw * cosines + pltpu.roll(query_raw, HEAD // 2, 1) * sines).astype(BF)
    grad_out = get(5)[...]
    scores = dot_nt(query, key) * factor
    scores = jnp.where(jnp.concatenate([get(3)[...]] * q_heads, 0) > 0.5, scores, F32(-1e30))
    exp_terms = jnp.exp(scores - jnp.max(scores, -1, keepdims=True))
    probs = exp_terms / jnp.sum(exp_terms, -1, keepdims=True)
    probs_low = probs.astype(BF)
    grad_probs = dot_nt(grad_out, value)
    mixed = dot_nn(probs_low, value).astype(BF)
    mixed = dot_nn(home, jnp.concatenate([mixed[at, :] for at in piles], 1)).astype(BF)
    for e in range(SLOTS):
        put(e)[...] = mixed[e * MAXLEN : (e + 1) * MAXLEN, :]
    grad_value = dot_tn(probs_low, grad_out)
    centre = jnp.sum(grad_probs * probs, -1, keepdims=True)
    grad_scores = (probs * (grad_probs - centre) * factor).astype(BF)
    grad_query = dot_nn(grad_scores, key)
    grad_key = dot_tn(grad_scores, query)
    grad_query = (grad_query * cosines - pltpu.roll(grad_query, HEAD // 2, 1) * sines).astype(BF)
    pile_dots = grad_query.astype(F32) * query_raw
    dots = jnp.zeros((TOK_DEV, HEAD), F32)
    for at, pile in zip(heads, piles):
        grads_ref[:, at] = grad_query[pile, :]
        dots = dots + pile_dots[pile, :]
    grad_key = (grad_key * cosine - pltpu.roll(grad_key, HEAD // 2, 1) * sine).astype(BF)
    grad_value = grad_value.astype(BF)
    grads_ref[:, kv_at : kv_at + HEAD] = grad_key
    grads_ref[:, kv_at + HEAD :] = grad_value
    value_out_ref[...] = grad_value
    dots = dots + grad_key.astype(F32) * key_raw + grad_value.astype(F32) * value_raw
    for e in range(SLOTS):
        send(e)
    share = jnp.sum(dots, 1, keepdims=True) / inverse
    share = jnp.transpose(jnp.broadcast_to(share, (TOK_DEV, TOK_DEV)))[0:EXTRA, :]
    high = share.astype(BF)
    low = (share - high.astype(F32)).astype(BF)
    tail = jnp.concatenate([high, low], 1)
    grads = grads_ref[...]
    for j in range(NZ):
        terms_ref[j, 2 * TOK_DEV :, :] = tail
        for half, ref in ((1 - c, 6), (c, 9)):
            at = pl.ds(pl.multiple_of(half * TOK_DEV, TOK_DEV), TOK_DEV)
            terms_ref[j, at, :] = dot_nt(grads, get(ref)[j * deep : (j + 1) * deep, :]).astype(BF)
        send(5, j)


def finish_kernel(get, put, send, smem, extra):
    packed_ref, inverse, total_ref = get(0), get(1)[:, 0:1], get(2)
    share = total_ref[2 * TOK_DEV :, :].astype(F32)
    share = share[0:1, :TOK_DEV] + share[0:1, TOK_DEV : 2 * TOK_DEV]
    row_dot = jnp.transpose(jnp.broadcast_to(share, (TOK_DEV, TOK_DEV)))[:, 0:1]
    row_dot = inverse * inverse * inverse * row_dot / D
    halves = []
    for h in range(2):
        gain = packed_ref[2 * TOK_DEV :, :].astype(F32)[h * (EXTRA // 2) : h * (EXTRA // 2) + 1, :]
        rows = slice(h * TOK_DEV, (h + 1) * TOK_DEV)
        weighted = total_ref[rows, :].astype(F32) * gain
        here = packed_ref[rows, :].astype(F32)
        halves.append((inverse * weighted - here * row_dot).astype(BF))
    grad = jnp.concatenate(halves, 1)
    put(0)[...] = dot_nt(grad, get(3)[...]).astype(BF)


def lay_kernel(get, put, send, smem, extra):
    rows = jnp.concatenate(
        [get(1 + e)[...] for e in range(SLOTS)], 0
    )
    put(0)[...] = dot_tn(get(0)[...], rows).astype(BF)


def kernel_call(body, outs, args, name, mib, scalars=0, scratch=(), cut_out=None):
    shapes = [jax.ShapeDtypeStruct(s, d) for s, d in outs]
    arrays = args[scalars:]
    n_in, n_out = len(arrays), len(shapes)
    n_cut = 0 if cut_out is None else shapes[cut_out].shape[0]

    def kernel(*refs):
        smem, refs = refs[:scalars], refs[scalars:]
        ins, refs = refs[:n_in], refs[n_in:]
        out, refs = refs[:n_out], refs[n_out:]
        in_buf, refs = refs[:n_in], refs[n_in:]
        out_buf, refs = refs[:n_out], refs[n_out:]
        in_sem, out_sem, extra = refs[0], refs[1], refs[2:]
        loads = [pltpu.make_async_copy(ins[i], in_buf[i], in_sem.at[i]) for i in range(n_in)]
        stores = {}
        for i in range(n_out):
            if i == cut_out:
                for j in range(shapes[i].shape[0]):
                    sem = out_sem.at[n_out + j]
                    stores[i, j] = pltpu.make_async_copy(out_buf[i].at[j], out[i].at[j], sem)
            else:
                stores[i, None] = pltpu.make_async_copy(out_buf[i], out[i], out_sem.at[i])
        for load in loads:
            load.start()
        waited, sent = set(), set()

        def get(i):
            if i not in waited:
                waited.add(i)
                loads[i].wait()
            return in_buf[i]

        def send(i, j=None):
            if (i, j) not in sent:
                sent.add((i, j))
                stores[i, j].start()

        body(get, lambda i: out_buf[i], send, smem, extra)
        for i in range(n_in):
            get(i)
        for i, j in stores:
            send(i, j)
        for store in stores.values():
            store.wait()

    hbm = pl.BlockSpec(memory_space=pltpu.HBM)
    return pl.pallas_call(
        kernel,
        out_shape=shapes,
        in_specs=[pl.BlockSpec(memory_space=pltpu.SMEM)] * scalars + [hbm] * n_in,
        out_specs=[hbm] * n_out,
        scratch_shapes=[pltpu.VMEM(v.shape, v.dtype) for v in arrays]
        + [pltpu.VMEM(v.shape, v.dtype) for v in shapes]
        + [pltpu.SemaphoreType.DMA((n_in,)), pltpu.SemaphoreType.DMA((n_out + n_cut,))]
        + list(scratch),
        compiler_params=pltpu.CompilerParams(vmem_limit_bytes=mib * MIB),
        name=name,
    )(*args)


def on_device(
    hidden, gain, w_query, w_key, w_value, cotangent, seq_length, home_offset, dest_shard, dest_offset
):
    shards = NZ * NX * NC
    peers = lax.axis_size("tensor")
    me, z, x, c = place()
    strides = [-1, 1, shards // 2, shards // 2 + 1]
    width = hidden.shape[1]
    deep = width // 2
    q_cols = w_query.shape[1]
    k_cols = w_key.shape[1]
    q_heads = q_cols // HEAD
    rows_each = D // shards

    own = jnp.concatenate([w_query, w_key, w_value], 1)
    own_half = lax.all_to_all(
        jnp.broadcast_to(own[None], (NX,) + own.shape), "x", split_axis=0, concat_axis=0, tiled=True
    ).reshape(NX * own.shape[0], own.shape[1])
    own_half, cotangent = tied(own_half, cotangent)
    mine = lax.all_gather(own_half, "z", axis=0, tiled=True)

    half = HEAD // 2
    freq = np.power(np.float32(ROPE_BASE), -(np.arange(half, dtype=np.float32) * np.float32(2.0 / HEAD)))
    freq = jnp.asarray(np.concatenate([freq, freq])[None, :].astype(np.float32))
    square = ((TOK_DEV, TOK_DEV), F32)
    block = (2 * TOK_DEV + EXTRA, deep)
    cut = ((MAXLEN, q_cols), BF)
    wide = ((2 * MAXLEN, q_cols), BF)
    cot_near, cot_behind, cot_far, home, dest, cosine, sine, allowed, packed, order = kernel_call(
        functools.partial(plan_kernel, strides, shards),
        [wide, cut, cut] + [((SLOTS * MAXLEN, TOK_DEV), BF), ((SLOTS * MAXLEN, CAP), BF)] + [square] * 3
        + [(block, BF), ((width, width), BF)],
        [seq_length.T, home_offset.T, dest_shard.T, dest_offset.T, freq, cotangent, hidden, gain[None, :]],
        "plan", 60, 4,
    )
    copies = jnp.broadcast_to(packed[None], (peers,) + packed.shape)
    rows_full = lax.all_to_all(copies, "tensor", split_axis=0, concat_axis=0, tiled=True)
    cot_near = passed_along(cot_near, -1)
    cot_behind = passed_along(cot_behind, 1)
    cot_far = passed_along(jnp.concatenate([cot_far, cot_near[MAXLEN:]], 0), shards // 2)

    mine, rows_full, cot_near, cot_behind, cot_far = tied(
        mine, rows_full, cot_near, cot_behind, cot_far
    )
    theirs = other_core(mine)

    normed, inverse, partial, grad_out = kernel_call(
        norm_kernel,
        [((2, TOK_DEV, NZ * deep), BF), square, ((TOK_DEV, q_cols + 2 * k_cols), F32), ((q_heads * TOK_DEV, HEAD), BF)],
        [rows_full, mine, home, cot_near, cot_behind, cot_far], "norm", 60,
    )
    *attn_cuts, grad_value, terms = kernel_call(
        functools.partial(layer_kernel, q_heads),
        [cut] * 4 + [((TOK_DEV, k_cols), BF), ((peers,) + block, BF)],
        [normed, cosine, sine, allowed, home, grad_out, theirs, inverse, partial, mine],
        "layer", 60, 0,
        [pltpu.VMEM((TOK_DEV, q_cols + 2 * k_cols), BF)], 5,
    )
    total = lax.psum_scatter(terms, "tensor", scatter_dimension=0, tiled=False)
    (grad_hidden,) = kernel_call(
        finish_kernel, [((TOK_DEV, width), BF)],
        [packed, inverse, total, order], "finish", 60,
    )

    share = ((NZ * NX, rows_each, k_cols), BF)
    kept, given = kernel_call(value_kernel, [share, share], [normed, grad_value], "value", 12)
    pair = (kept.astype(F32) + other_core(given).astype(F32)).astype(BF)
    parts = lax.all_to_all(pair, ("z", "x"), split_axis=0, concat_axis=0, tiled=True)
    grad_value_weight = jnp.sum(parts.astype(F32), 0)

    attn_sent = [passed_along(attn_cuts[n], s) for n, s in enumerate(strides)]
    (attn_out,) = kernel_call(
        lay_kernel, [((CAP, q_cols), BF)], [dest, *attn_sent], "lay", 8
    )
    return (attn_out, grad_hidden, grad_value_weight)


def solution(mesh):
    fine = Mesh(mesh.devices.reshape(NZ, NX, NC, -1), DP + ("tensor",))
    both = P(DP, "tensor")
    return jax.shard_map(
        on_device,
        mesh=fine,
        in_specs=(both, P("tensor")) + (both,) * 4 + (P(),) * 4,
        out_specs=(both,) * 3,
        check_vma=False,
    )
```

```python
import functools

import jax
import jax.numpy as jnp
import numpy as np
from jax import lax
from jax.experimental import pallas as pl
from jax.experimental.pallas import tpu as pltpu
from jax.sharding import Mesh, PartitionSpec as P

D = 4096
HEAD = 128
TOK_DEV = 128
MAXLEN = 64
CAP = 256
SLOTS = 4
EXTRA = 16
EPSILON = 1e-05
ROPE_BASE = 500000.0
NZ, NX, NC = 8, 4, 2
DP = ("z", "x", "core")
BF = jnp.bfloat16
F32 = jnp.float32
MIB = 1024 * 1024


def moved(value, where):
    pairs = []
    for z in range(NZ):
        for x in range(NX):
            for c in range(NC):
                tz, tx, tc = where(z, x, c)
                pairs.append(((z * NX + x) * NC + c, ((tz % NZ) * NX + tx % NX) * NC + tc))
    return lax.ppermute(value, DP, pairs)


def other_core(value):
    return moved(value, lambda z, x, c: (z, x, 1 - c))


def passed_along(value, by):
    size = NZ * NX * NC
    return lax.ppermute(value, DP, [(i, (i + by) % size) for i in range(size)])


def tied(*values):
    return lax.optimization_barrier(values)


def dot_nn(a, b):
    return lax.dot_general(a, b, (((1,), (0,)), ((), ())), preferred_element_type=F32)


def dot_nt(a, b):
    return lax.dot_general(a, b, (((1,), (1,)), ((), ())), preferred_element_type=F32)


def dot_tn(a, b):
    return lax.dot_general(a, b, (((0,), (0,)), ((), ())), preferred_element_type=F32)


def place():
    z, x, c = [lax.axis_index(axis) for axis in DP]
    return (z * NX + x) * NC + c, z, x, c


def feature_order(width):
    natural = lax.broadcasted_iota(jnp.int32, (width, width), 0)
    place_in = lax.broadcasted_iota(jnp.int32, (width, width), 1)
    core = place_in >> 8
    x = (place_in >> 6) & (NX - 1)
    return jnp.where(natural == x * (NC * 64) + core * 64 + (place_in & 63), 1.0, 0.0).astype(BF)


def plan_kernel(
    strides, shards, get, put, send, smem, extra,
):
    len_ref, off_ref, shard_ref, start_ref = smem
    home_ref, dest_ref, cos_ref, sin_ref, allowed_ref, packed_ref = [put(3 + i) for i in range(6)]
    deep = packed_ref.shape[1]
    order = feature_order(2 * deep)
    features = dot_nn(get(2)[...], order).astype(BF)
    gains = dot_nn(jnp.broadcast_to(get(3)[...], (EXTRA, 2 * deep)), order)
    for h in range(2):
        packed_ref[h * TOK_DEV : (h + 1) * TOK_DEV, :] = features[:, h * deep : (h + 1) * deep]
    gains = jnp.concatenate(
        [gains[: EXTRA // 2, :deep], gains[: EXTRA // 2, deep:]], 0
    )
    packed_ref[2 * TOK_DEV :, :] = gains.astype(BF)
    send(8)
    put(9)[...] = order
    send(9)
    me = place()[0]
    rows = lax.broadcasted_iota(jnp.int32, (TOK_DEV, TOK_DEV), 0)
    cols = lax.broadcasted_iota(jnp.int32, (TOK_DEV, TOK_DEV), 1)
    row_seq, row_pos = jnp.zeros_like(rows), jnp.zeros_like(rows)
    col_seq, col_pos = jnp.zeros_like(rows), jnp.zeros_like(rows)
    for e, stride in enumerate(strides):
        target = lax.rem(me + stride + shards, shards)
        source = lax.rem(me - stride + shards, shards)
        length = jnp.int32(0)
        offset = jnp.int32(0)
        in_len = jnp.int32(0)
        in_start = jnp.int32(0)
        for c in range(SLOTS):
            mine = shard_ref[c, me] == target
            length = length + jnp.where(mine, len_ref[c, me], 0)
            offset = offset + jnp.where(mine, off_ref[c, me], 0)
            theirs = shard_ref[c, source] == me
            in_len = in_len + jnp.where(theirs, len_ref[c, source], 0)
            in_start = in_start + jnp.where(theirs, start_ref[c, source], 0)
        inside = (rows >= offset) & (rows < offset + length)
        row_seq = jnp.where(inside, e, row_seq)
        row_pos = jnp.where(inside, rows - offset, row_pos)
        inside = (cols >= offset) & (cols < offset + length)
        col_seq = jnp.where(inside, e, col_seq)
        col_pos = jnp.where(inside, cols - offset, col_pos)
        at = slice(e * MAXLEN, (e + 1) * MAXLEN)
        t = lax.broadcasted_iota(jnp.int32, (MAXLEN, TOK_DEV), 0)
        r = lax.broadcasted_iota(jnp.int32, (MAXLEN, TOK_DEV), 1)
        home_ref[at, :] = jnp.where((r == t + offset) & (t < length), 1.0, 0.0).astype(BF)
        t = lax.broadcasted_iota(jnp.int32, (MAXLEN, CAP), 0)
        r = lax.broadcasted_iota(jnp.int32, (MAXLEN, CAP), 1)
        dest = jnp.where((r == t + in_start) & (t < in_len), 1.0, 0.0).astype(BF)
        dest_ref[at, :] = dest
        ref, lo = ((1, 0), (0, 0), (2, 0), (0, MAXLEN))[e]
        put(ref)[lo : lo + MAXLEN, :] = dot_nn(dest, get(1)[...]).astype(BF)
    allowed_ref[...] = jnp.where((row_seq == col_seq) & (col_pos <= row_pos), 1.0, 0.0)
    angles = row_pos.astype(F32) * get(0)[...]
    cos_ref[...] = jnp.cos(angles)
    sine = jnp.sin(angles)
    sin_ref[...] = jnp.where(cols < HEAD // 2, -sine, sine)


def norm_kernel(get, put, send, smem, extra):
    c = place()[3]
    rows_ref, normed_ref, inverse_ref, partial_ref = get(0), put(0), put(1), put(2)
    cot = jnp.concatenate([get(4)[...], get(3)[:MAXLEN, :], get(5)[...]], 0)
    cot = dot_tn(get(2)[...], cot).astype(BF)
    for g in range(cot.shape[1] // HEAD):
        put(3)[g * TOK_DEV : (g + 1) * TOK_DEV, :] = cot[:, g * HEAD : (g + 1) * HEAD]
    send(3)
    deep = rows_ref.shape[2]
    squares = jnp.zeros((TOK_DEV, 1), F32)
    for j in range(NZ):
        for h in range(2):
            part = rows_ref[j, h * TOK_DEV : (h + 1) * TOK_DEV, :].astype(F32)
            squares = squares + jnp.sum(part * part, 1, keepdims=True)
    inverse = lax.rsqrt(squares / D + EPSILON)
    inverse_ref[...] = jnp.broadcast_to(inverse, inverse_ref.shape)
    for n, half in enumerate((c, 1 - c)):
        for j in range(NZ):
            gains = rows_ref[j, 2 * TOK_DEV :, :].astype(F32)
            gain = jnp.where(half == 0, gains[0:1, :], gains[EXTRA // 2 : EXTRA // 2 + 1, :])
            at = pl.ds(pl.multiple_of(half * TOK_DEV, TOK_DEV), TOK_DEV)
            part = rows_ref[j, at, :].astype(F32) * inverse * gain
            normed_ref[n, :, j * deep : (j + 1) * deep] = part.astype(BF)
    send(0)
    partial_ref[...] = dot_nn(normed_ref[0], get(1)[...])


def value_kernel(get, put, send, smem, extra):
    kept_ref, given_ref = put(0), put(1)
    grad_value = get(1)[...]
    for n, ref in enumerate((kept_ref, given_ref)):
        for j in range(NZ):
            found = dot_tn(get(0)[n, :, j * 256 : (j + 1) * 256], grad_value).astype(BF)
            for x in range(NX):
                ref[j * NX + x] = found[x * 64 : (x + 1) * 64, :]


def layer_kernel(q_heads, get, put, send, smem, extra):
    (grads_ref,) = extra
    value_out_ref, terms_ref = put(4), put(5)
    c = place()[3]
    kv_at = q_heads * HEAD
    inverse = get(7)[:, 0:1]
    deep = terms_ref.shape[2]
    projected = get(8)[...] + dot_nn(get(0)[1], get(6)[...])
    cosine = get(1)[...]
    sine = get(2)[...]
    factor = HEAD ** (-0.5)
    home = get(4)[...]
    key_raw = projected[:, kv_at : kv_at + HEAD]
    value_raw = projected[:, kv_at + HEAD :]
    key = (key_raw * cosine + pltpu.roll(key_raw, HEAD // 2, 1) * sine).astype(BF)
    value = value_raw.astype(BF)
    heads = [slice(g * HEAD, (g + 1) * HEAD) for g in range(q_heads)]
    piles = [slice(g * TOK_DEV, (g + 1) * TOK_DEV) for g in range(q_heads)]
    cosines = jnp.concatenate([cosine] * q_heads, 0)
    sines = jnp.concatenate([sine] * q_heads, 0)
    query_raw = jnp.concatenate([projected[:, at] for at in heads], 0)
    query = (query_raw * cosines + pltpu.roll(query_raw, HEAD // 2, 1) * sines).astype(BF)
    grad_out = get(5)[...]
    scores = dot_nt(query, key) * factor
    scores = jnp.where(jnp.concatenate([get(3)[...]] * q_heads, 0) > 0.5, scores, F32(-1e30))
    exp_terms = jnp.exp(scores - jnp.max(scores, -1, keepdims=True))
    probs = exp_terms / jnp.sum(exp_terms, -1, keepdims=True)
    probs_low = probs.astype(BF)
    grad_probs = dot_nt(grad_out, value)
    mixed = dot_nn(probs_low, value).astype(BF)
    mixed = dot_nn(home, jnp.concatenate([mixed[at, :] for at in piles], 1)).astype(BF)
    for e in range(SLOTS):
        put(e)[...] = mixed[e * MAXLEN : (e + 1) * MAXLEN, :]
    grad_value = dot_tn(probs_low, grad_out)
    centre = jnp.sum(grad_probs * probs, -1, keepdims=True)
    grad_scores = (probs * (grad_probs - centre) * factor).astype(BF)
    grad_query = dot_nn(grad_scores, key)
    grad_key = dot_tn(grad_scores, query)
    grad_query = (grad_query * cosines - pltpu.roll(grad_query, HEAD // 2, 1) * sines).astype(BF)
    pile_dots = grad_query.astype(F32) * query_raw
    dots = jnp.zeros((TOK_DEV, HEAD), F32)
    for at, pile in zip(heads, piles):
        grads_ref[:, at] = grad_query[pile, :]
        dots = dots + pile_dots[pile, :]
    grad_key = (grad_key * cosine - pltpu.roll(grad_key, HEAD // 2, 1) * sine).astype(BF)
    grad_value = grad_value.astype(BF)
    grads_ref[:, kv_at : kv_at + HEAD] = grad_key
    grads_ref[:, kv_at + HEAD :] = grad_value
    value_out_ref[...] = grad_value
    dots = dots + grad_key.astype(F32) * key_raw + grad_value.astype(F32) * value_raw
    for e in range(SLOTS):
        send(e)
    share = jnp.sum(dots, 1, keepdims=True) / inverse
    share = jnp.transpose(jnp.broadcast_to(share, (TOK_DEV, TOK_DEV)))[0:EXTRA, :]
    high = share.astype(BF)
    low = (share - high.astype(F32)).astype(BF)
    tail = jnp.concatenate([high, low], 1)
    grads = grads_ref[...]
    for j in range(NZ):
        terms_ref[j, 2 * TOK_DEV :, :] = tail
        for half, ref in ((1 - c, 6), (c, 9)):
            at = pl.ds(pl.multiple_of(half * TOK_DEV, TOK_DEV), TOK_DEV)
            terms_ref[j, at, :] = dot_nt(grads, get(ref)[j * deep : (j + 1) * deep, :]).astype(BF)
        send(5, j)


def finish_kernel(get, put, send, smem, extra):
    packed_ref, inverse, total_ref = get(0), get(1)[:, 0:1], get(2)
    share = total_ref[2 * TOK_DEV :, :].astype(F32)
    share = share[0:1, :TOK_DEV] + share[0:1, TOK_DEV : 2 * TOK_DEV]
    row_dot = jnp.transpose(jnp.broadcast_to(share, (TOK_DEV, TOK_DEV)))[:, 0:1]
    row_dot = inverse * inverse * inverse * row_dot / D
    halves = []
    for h in range(2):
        gain = packed_ref[2 * TOK_DEV :, :].astype(F32)[h * (EXTRA // 2) : h * (EXTRA // 2) + 1, :]
        rows = slice(h * TOK_DEV, (h + 1) * TOK_DEV)
        weighted = total_ref[rows, :].astype(F32) * gain
        here = packed_ref[rows, :].astype(F32)
        halves.append((inverse * weighted - here * row_dot).astype(BF))
    grad = jnp.concatenate(halves, 1)
    put(0)[...] = dot_nt(grad, get(3)[...]).astype(BF)


def lay_kernel(get, put, send, smem, extra):
    rows = jnp.concatenate(
        [get(1 + e)[...] for e in range(SLOTS)], 0
    )
    put(0)[...] = dot_tn(get(0)[...], rows).astype(BF)


def kernel_call(body, outs, args, name, mib, scalars=0, scratch=(), cut_out=None):
    shapes = [jax.ShapeDtypeStruct(s, d) for s, d in outs]
    arrays = args[scalars:]
    n_in, n_out = len(arrays), len(shapes)
    n_cut = 0 if cut_out is None else shapes[cut_out].shape[0]

    def kernel(*refs):
        smem, refs = refs[:scalars], refs[scalars:]
        ins, refs = refs[:n_in], refs[n_in:]
        out, refs = refs[:n_out], refs[n_out:]
        in_buf, refs = refs[:n_in], refs[n_in:]
        out_buf, refs = refs[:n_out], refs[n_out:]
        in_sem, out_sem, extra = refs[0], refs[1], refs[2:]
        loads = [pltpu.make_async_copy(ins[i], in_buf[i], in_sem.at[i]) for i in range(n_in)]
        stores = {}
        for i in range(n_out):
            if i == cut_out:
                for j in range(shapes[i].shape[0]):
                    sem = out_sem.at[n_out + j]
                    stores[i, j] = pltpu.make_async_copy(out_buf[i].at[j], out[i].at[j], sem)
            else:
                stores[i, None] = pltpu.make_async_copy(out_buf[i], out[i], out_sem.at[i])
        for load in loads:
            load.start()
        waited, sent = set(), set()

        def get(i):
            if i not in waited:
                waited.add(i)
                loads[i].wait()
            return in_buf[i]

        def send(i, j=None):
            if (i, j) not in sent:
                sent.add((i, j))
                stores[i, j].start()

        body(get, lambda i: out_buf[i], send, smem, extra)
        for i in range(n_in):
            get(i)
        for i, j in stores:
            send(i, j)
        for store in stores.values():
            store.wait()

    hbm = pl.BlockSpec(memory_space=pltpu.HBM)
    return pl.pallas_call(
        kernel,
        out_shape=shapes,
        in_specs=[pl.BlockSpec(memory_space=pltpu.SMEM)] * scalars + [hbm] * n_in,
        out_specs=[hbm] * n_out,
        scratch_shapes=[pltpu.VMEM(v.shape, v.dtype) for v in arrays]
        + [pltpu.VMEM(v.shape, v.dtype) for v in shapes]
        + [pltpu.SemaphoreType.DMA((n_in,)), pltpu.SemaphoreType.DMA((n_out + n_cut,))]
        + list(scratch),
        compiler_params=pltpu.CompilerParams(vmem_limit_bytes=mib * MIB),
        name=name,
    )(*args)


def on_device(
    hidden, gain, w_query, w_key, w_value, cotangent, seq_length, home_offset, dest_shard, dest_offset
):
    shards = NZ * NX * NC
    peers = lax.axis_size("tensor")
    me, z, x, c = place()
    strides = [-1, 1, shards // 2, shards // 2 + 1]
    width = hidden.shape[1]
    deep = width // 2
    q_cols = w_query.shape[1]
    k_cols = w_key.shape[1]
    q_heads = q_cols // HEAD
    rows_each = D // shards

    own = jnp.concatenate([w_query, w_key, w_value], 1)
    own_half = lax.all_to_all(
        jnp.broadcast_to(own[None], (NX,) + own.shape), "x", split_axis=0, concat_axis=0, tiled=True
    ).reshape(NX * own.shape[0], own.shape[1])
    own_half, cotangent = tied(own_half, cotangent)
    mine = lax.all_gather(own_half, "z", axis=0, tiled=True)

    half = HEAD // 2
    freq = np.power(np.float32(ROPE_BASE), -(np.arange(half, dtype=np.float32) * np.float32(2.0 / HEAD)))
    freq = jnp.asarray(np.concatenate([freq, freq])[None, :].astype(np.float32))
    square = ((TOK_DEV, TOK_DEV), F32)
    block = (2 * TOK_DEV + EXTRA, deep)
    cut = ((MAXLEN, q_cols), BF)
    wide = ((2 * MAXLEN, q_cols), BF)
    cot_near, cot_behind, cot_far, home, dest, cosine, sine, allowed, packed, order = kernel_call(
        functools.partial(plan_kernel, strides, shards),
        [wide, cut, cut] + [((SLOTS * MAXLEN, TOK_DEV), BF), ((SLOTS * MAXLEN, CAP), BF)] + [square] * 3
        + [(block, BF), ((width, width), BF)],
        [seq_length.T, home_offset.T, dest_shard.T, dest_offset.T, freq, cotangent, hidden, gain[None, :]],
        "plan", 60, 4,
    )
    copies = jnp.broadcast_to(packed[None], (peers,) + packed.shape)
    rows_full = lax.all_to_all(copies, "tensor", split_axis=0, concat_axis=0, tiled=True)
    cot_near = passed_along(cot_near, -1)
    cot_behind = passed_along(cot_behind, 1)
    cot_far = passed_along(jnp.concatenate([cot_far, cot_near[MAXLEN:]], 0), shards // 2)

    mine, rows_full, cot_near, cot_behind, cot_far = tied(
        mine, rows_full, cot_near, cot_behind, cot_far
    )
    theirs = other_core(mine)

    normed, inverse, partial, grad_out = kernel_call(
        norm_kernel,
        [((2, TOK_DEV, NZ * deep), BF), square, ((TOK_DEV, q_cols + 2 * k_cols), F32), ((q_heads * TOK_DEV, HEAD), BF)],
        [rows_full, mine, home, cot_near, cot_behind, cot_far], "norm", 60,
    )
    *attn_cuts, grad_value, terms = kernel_call(
        functools.partial(layer_kernel, q_heads),
        [cut] * 4 + [((TOK_DEV, k_cols), BF), ((peers,) + block, BF)],
        [normed, cosine, sine, allowed, home, grad_out, theirs, inverse, partial, mine],
        "layer", 50, 0,
        [pltpu.VMEM((TOK_DEV, q_cols + 2 * k_cols), BF)], 5,
    )
    total = lax.psum_scatter(terms, "tensor", scatter_dimension=0, tiled=False)
    (grad_hidden,) = kernel_call(
        finish_kernel, [((TOK_DEV, width), BF)],
        [packed, inverse, total, order], "finish", 60,
    )

    share = ((NZ * NX, rows_each, k_cols), BF)
    kept, given = kernel_call(value_kernel, [share, share], [normed, grad_value], "value", 12)
    pair = (kept.astype(F32) + other_core(given).astype(F32)).astype(BF)
    parts = lax.all_to_all(pair, ("z", "x"), split_axis=0, concat_axis=0, tiled=True)
    grad_value_weight = jnp.sum(parts.astype(F32), 0)

    attn_sent = [passed_along(attn_cuts[n], s) for n, s in enumerate(strides)]
    (attn_out,) = kernel_call(
        lay_kernel, [((CAP, q_cols), BF)], [dest, *attn_sent], "lay", 8
    )
    return (attn_out, grad_hidden, grad_value_weight)


def solution(mesh):
    fine = Mesh(mesh.devices.reshape(NZ, NX, NC, -1), DP + ("tensor",))
    both = P(DP, "tensor")
    return jax.shard_map(
        on_device,
        mesh=fine,
        in_specs=(both, P("tensor")) + (both,) * 4 + (P(),) * 4,
        out_specs=(both,) * 3,
        check_vma=False,
    )
```

```python
import functools

import jax
import jax.numpy as jnp
import numpy as np
from jax import lax
from jax.experimental import pallas as pl
from jax.experimental.pallas import tpu as pltpu
from jax.sharding import Mesh, PartitionSpec as P

D = 4096
HEAD = 128
TOK_DEV = 128
MAXLEN = 64
CAP = 256
SLOTS = 4
EXTRA = 16
EPSILON = 1e-05
ROPE_BASE = 500000.0
NZ, NX, NC = 8, 4, 2
DP = ("z", "x", "core")
BF = jnp.bfloat16
F32 = jnp.float32
MIB = 1024 * 1024


def moved(value, where):
    pairs = []
    for z in range(NZ):
        for x in range(NX):
            for c in range(NC):
                tz, tx, tc = where(z, x, c)
                pairs.append(((z * NX + x) * NC + c, ((tz % NZ) * NX + tx % NX) * NC + tc))
    return lax.ppermute(value, DP, pairs)


def other_core(value):
    return moved(value, lambda z, x, c: (z, x, 1 - c))


def passed_along(value, by):
    size = NZ * NX * NC
    return lax.ppermute(value, DP, [(i, (i + by) % size) for i in range(size)])


def tied(*values):
    return lax.optimization_barrier(values)


def dot_nn(a, b):
    return lax.dot_general(a, b, (((1,), (0,)), ((), ())), preferred_element_type=F32)


def dot_nt(a, b):
    return lax.dot_general(a, b, (((1,), (1,)), ((), ())), preferred_element_type=F32)


def dot_tn(a, b):
    return lax.dot_general(a, b, (((0,), (0,)), ((), ())), preferred_element_type=F32)


def place():
    z, x, c = [lax.axis_index(axis) for axis in DP]
    return (z * NX + x) * NC + c, z, x, c


def feature_order(width):
    natural = lax.broadcasted_iota(jnp.int32, (width, width), 0)
    place_in = lax.broadcasted_iota(jnp.int32, (width, width), 1)
    core = place_in >> 8
    x = (place_in >> 6) & (NX - 1)
    return jnp.where(natural == x * (NC * 64) + core * 64 + (place_in & 63), 1.0, 0.0).astype(BF)


def plan_kernel(
    strides, shards, get, put, send, smem, extra,
):
    len_ref, off_ref, shard_ref, start_ref = smem
    home_ref, dest_ref, cos_ref, sin_ref, allowed_ref, packed_ref = [put(3 + i) for i in range(6)]
    deep = packed_ref.shape[1]
    order = feature_order(2 * deep)
    features = dot_nn(get(2)[...], order).astype(BF)
    gains = dot_nn(jnp.broadcast_to(get(3)[...], (EXTRA, 2 * deep)), order)
    for h in range(2):
        packed_ref[h * TOK_DEV : (h + 1) * TOK_DEV, :] = features[:, h * deep : (h + 1) * deep]
    gains = jnp.concatenate(
        [gains[: EXTRA // 2, :deep], gains[: EXTRA // 2, deep:]], 0
    )
    packed_ref[2 * TOK_DEV :, :] = gains.astype(BF)
    send(8)
    put(9)[...] = order
    send(9)
    me = place()[0]
    rows = lax.broadcasted_iota(jnp.int32, (TOK_DEV, TOK_DEV), 0)
    cols = lax.broadcasted_iota(jnp.int32, (TOK_DEV, TOK_DEV), 1)
    row_seq, row_pos = jnp.zeros_like(rows), jnp.zeros_like(rows)
    col_seq, col_pos = jnp.zeros_like(rows), jnp.zeros_like(rows)
    for e, stride in enumerate(strides):
        target = lax.rem(me + stride + shards, shards)
        source = lax.rem(me - stride + shards, shards)
        length = jnp.int32(0)
        offset = jnp.int32(0)
        in_len = jnp.int32(0)
        in_start = jnp.int32(0)
        for c in range(SLOTS):
            mine = shard_ref[c, me] == target
            length = length + jnp.where(mine, len_ref[c, me], 0)
            offset = offset + jnp.where(mine, off_ref[c, me], 0)
            theirs = shard_ref[c, source] == me
            in_len = in_len + jnp.where(theirs, len_ref[c, source], 0)
            in_start = in_start + jnp.where(theirs, start_ref[c, source], 0)
        inside = (rows >= offset) & (rows < offset + length)
        row_seq = jnp.where(inside, e, row_seq)
        row_pos = jnp.where(inside, rows - offset, row_pos)
        inside = (cols >= offset) & (cols < offset + length)
        col_seq = jnp.where(inside, e, col_seq)
        col_pos = jnp.where(inside, cols - offset, col_pos)
        at = slice(e * MAXLEN, (e + 1) * MAXLEN)
        t = lax.broadcasted_iota(jnp.int32, (MAXLEN, TOK_DEV), 0)
        r = lax.broadcasted_iota(jnp.int32, (MAXLEN, TOK_DEV), 1)
        home_ref[at, :] = jnp.where((r == t + offset) & (t < length), 1.0, 0.0).astype(BF)
        t = lax.broadcasted_iota(jnp.int32, (MAXLEN, CAP), 0)
        r = lax.broadcasted_iota(jnp.int32, (MAXLEN, CAP), 1)
        dest = jnp.where((r == t + in_start) & (t < in_len), 1.0, 0.0).astype(BF)
        dest_ref[at, :] = dest
        ref, lo = ((1, 0), (0, 0), (2, 0), (0, MAXLEN))[e]
        put(ref)[lo : lo + MAXLEN, :] = dot_nn(dest, get(1)[...]).astype(BF)
    allowed_ref[...] = jnp.where((row_seq == col_seq) & (col_pos <= row_pos), 1.0, 0.0)
    angles = row_pos.astype(F32) * get(0)[...]
    cos_ref[...] = jnp.cos(angles)
    sine = jnp.sin(angles)
    sin_ref[...] = jnp.where(cols < HEAD // 2, -sine, sine)


def norm_kernel(get, put, send, smem, extra):
    c = place()[3]
    rows_ref, normed_ref, inverse_ref, partial_ref = get(0), put(0), put(1), put(2)
    cot = jnp.concatenate([get(4)[...], get(3)[:MAXLEN, :], get(5)[...]], 0)
    cot = dot_tn(get(2)[...], cot).astype(BF)
    for g in range(cot.shape[1] // HEAD):
        put(3)[g * TOK_DEV : (g + 1) * TOK_DEV, :] = cot[:, g * HEAD : (g + 1) * HEAD]
    send(3)
    deep = rows_ref.shape[2]
    squares = jnp.zeros((TOK_DEV, 1), F32)
    for j in range(NZ):
        for h in range(2):
            part = rows_ref[j, h * TOK_DEV : (h + 1) * TOK_DEV, :].astype(F32)
            squares = squares + jnp.sum(part * part, 1, keepdims=True)
    inverse = lax.rsqrt(squares / D + EPSILON)
    inverse_ref[...] = jnp.broadcast_to(inverse, inverse_ref.shape)
    for n, half in enumerate((c, 1 - c)):
        for j in range(NZ):
            gains = rows_ref[j, 2 * TOK_DEV :, :].astype(F32)
            gain = jnp.where(half == 0, gains[0:1, :], gains[EXTRA // 2 : EXTRA // 2 + 1, :])
            at = pl.ds(pl.multiple_of(half * TOK_DEV, TOK_DEV), TOK_DEV)
            part = rows_ref[j, at, :].astype(F32) * inverse * gain
            normed_ref[n, :, j * deep : (j + 1) * deep] = part.astype(BF)
    send(0)
    partial_ref[...] = dot_nn(normed_ref[0], get(1)[...])


def value_kernel(get, put, send, smem, extra):
    kept_ref, given_ref = put(0), put(1)
    grad_value = get(1)[...]
    for n, ref in enumerate((kept_ref, given_ref)):
        for j in range(NZ):
            found = dot_tn(get(0)[n, :, j * 256 : (j + 1) * 256], grad_value).astype(BF)
            for x in range(NX):
                ref[j * NX + x] = found[x * 64 : (x + 1) * 64, :]


def layer_kernel(q_heads, get, put, send, smem, extra):
    (grads_ref,) = extra
    value_out_ref, terms_ref = put(4), put(5)
    c = place()[3]
    kv_at = q_heads * HEAD
    inverse = get(7)[:, 0:1]
    deep = terms_ref.shape[2]
    projected = get(8)[...] + dot_nn(get(0)[1], get(6)[...])
    cosine = get(1)[...]
    sine = get(2)[...]
    factor = HEAD ** (-0.5)
    home = get(4)[...]
    key_raw = projected[:, kv_at : kv_at + HEAD]
    value_raw = projected[:, kv_at + HEAD :]
    key = (key_raw * cosine + pltpu.roll(key_raw, HEAD // 2, 1) * sine).astype(BF)
    value = value_raw.astype(BF)
    heads = [slice(g * HEAD, (g + 1) * HEAD) for g in range(q_heads)]
    piles = [slice(g * TOK_DEV, (g + 1) * TOK_DEV) for g in range(q_heads)]
    cosines = jnp.concatenate([cosine] * q_heads, 0)
    sines = jnp.concatenate([sine] * q_heads, 0)
    query_raw = jnp.concatenate([projected[:, at] for at in heads], 0)
    query = (query_raw * cosines + pltpu.roll(query_raw, HEAD // 2, 1) * sines).astype(BF)
    grad_out = get(5)[...]
    scores = dot_nt(query, key) * factor
    scores = jnp.where(jnp.concatenate([get(3)[...]] * q_heads, 0) > 0.5, scores, F32(-1e30))
    exp_terms = jnp.exp(scores - jnp.max(scores, -1, keepdims=True))
    probs = exp_terms / jnp.sum(exp_terms, -1, keepdims=True)
    probs_low = probs.astype(BF)
    grad_probs = dot_nt(grad_out, value)
    mixed = dot_nn(probs_low, value).astype(BF)
    mixed = dot_nn(home, jnp.concatenate([mixed[at, :] for at in piles], 1)).astype(BF)
    for e in range(SLOTS):
        put(e)[...] = mixed[e * MAXLEN : (e + 1) * MAXLEN, :]
    grad_value = dot_tn(probs_low, grad_out)
    centre = jnp.sum(grad_probs * probs, -1, keepdims=True)
    grad_scores = (probs * (grad_probs - centre) * factor).astype(BF)
    grad_query = dot_nn(grad_scores, key)
    grad_key = dot_tn(grad_scores, query)
    grad_query = (grad_query * cosines - pltpu.roll(grad_query, HEAD // 2, 1) * sines).astype(BF)
    pile_dots = grad_query.astype(F32) * query_raw
    dots = jnp.zeros((TOK_DEV, HEAD), F32)
    for at, pile in zip(heads, piles):
        grads_ref[:, at] = grad_query[pile, :]
        dots = dots + pile_dots[pile, :]
    grad_key = (grad_key * cosine - pltpu.roll(grad_key, HEAD // 2, 1) * sine).astype(BF)
    grad_value = grad_value.astype(BF)
    grads_ref[:, kv_at : kv_at + HEAD] = grad_key
    grads_ref[:, kv_at + HEAD :] = grad_value
    value_out_ref[...] = grad_value
    dots = dots + grad_key.astype(F32) * key_raw + grad_value.astype(F32) * value_raw
    for e in range(SLOTS):
        send(e)
    share = jnp.sum(dots, 1, keepdims=True) / inverse
    share = jnp.transpose(jnp.broadcast_to(share, (TOK_DEV, TOK_DEV)))[0:EXTRA, :]
    high = share.astype(BF)
    low = (share - high.astype(F32)).astype(BF)
    tail = jnp.concatenate([high, low], 1)
    grads = grads_ref[...]
    for j in range(NZ):
        terms_ref[j, 2 * TOK_DEV :, :] = tail
        for half, ref in ((1 - c, 6), (c, 9)):
            at = pl.ds(pl.multiple_of(half * TOK_DEV, TOK_DEV), TOK_DEV)
            terms_ref[j, at, :] = dot_nt(grads, get(ref)[j * deep : (j + 1) * deep, :]).astype(BF)
        send(5, j)


def finish_kernel(get, put, send, smem, extra):
    packed_ref, inverse, total_ref = get(0), get(1)[:, 0:1], get(2)
    share = total_ref[2 * TOK_DEV :, :].astype(F32)
    share = share[0:1, :TOK_DEV] + share[0:1, TOK_DEV : 2 * TOK_DEV]
    row_dot = jnp.transpose(jnp.broadcast_to(share, (TOK_DEV, TOK_DEV)))[:, 0:1]
    row_dot = inverse * inverse * inverse * row_dot / D
    halves = []
    for h in range(2):
        gain = packed_ref[2 * TOK_DEV :, :].astype(F32)[h * (EXTRA // 2) : h * (EXTRA // 2) + 1, :]
        rows = slice(h * TOK_DEV, (h + 1) * TOK_DEV)
        weighted = total_ref[rows, :].astype(F32) * gain
        here = packed_ref[rows, :].astype(F32)
        halves.append((inverse * weighted - here * row_dot).astype(BF))
    grad = jnp.concatenate(halves, 1)
    put(0)[...] = dot_nt(grad, get(3)[...]).astype(BF)


def lay_kernel(get, put, send, smem, extra):
    rows = jnp.concatenate(
        [get(1 + e)[...] for e in range(SLOTS)], 0
    )
    put(0)[...] = dot_tn(get(0)[...], rows).astype(BF)


def kernel_call(body, outs, args, name, mib, scalars=0, scratch=(), cut_out=None, late=None):
    shapes = [jax.ShapeDtypeStruct(s, d) for s, d in outs]
    arrays = args[scalars:]
    n_in, n_out = len(arrays), len(shapes)
    n_cut = 0 if cut_out is None else shapes[cut_out].shape[0]

    def kernel(*refs):
        smem, refs = refs[:scalars], refs[scalars:]
        ins, refs = refs[:n_in], refs[n_in:]
        out, refs = refs[:n_out], refs[n_out:]
        in_buf, refs = refs[:n_in], refs[n_in:]
        out_buf, refs = refs[:n_out], refs[n_out:]
        in_sem, out_sem, extra = refs[0], refs[1], refs[2:]
        loads = [pltpu.make_async_copy(ins[i], in_buf[i], in_sem.at[i]) for i in range(n_in)]
        stores = {}
        for i in range(n_out):
            if i == cut_out:
                for j in range(shapes[i].shape[0]):
                    sem = out_sem.at[n_out + j]
                    stores[i, j] = pltpu.make_async_copy(out_buf[i].at[j], out[i].at[j], sem)
            else:
                stores[i, None] = pltpu.make_async_copy(out_buf[i], out[i], out_sem.at[i])
        begin = list(range(n_in))
        if late is not None:
            begin.remove(late[1])
            begin.remove(late[0])
            begin.insert(0, late[0])
        for i in begin:
            loads[i].start()
        waited, sent = set(), set()

        def get(i):
            if i not in waited:
                waited.add(i)
                loads[i].wait()
                if late is not None and i == late[0]:
                    loads[late[1]].start()
            return in_buf[i]

        def send(i, j=None):
            if (i, j) not in sent:
                sent.add((i, j))
                stores[i, j].start()

        body(get, lambda i: out_buf[i], send, smem, extra)
        for i in range(n_in):
            get(i)
        for i, j in stores:
            send(i, j)
        for store in stores.values():
            store.wait()

    hbm = pl.BlockSpec(memory_space=pltpu.HBM)
    return pl.pallas_call(
        kernel,
        out_shape=shapes,
        in_specs=[pl.BlockSpec(memory_space=pltpu.SMEM)] * scalars + [hbm] * n_in,
        out_specs=[hbm] * n_out,
        scratch_shapes=[pltpu.VMEM(v.shape, v.dtype) for v in arrays]
        + [pltpu.VMEM(v.shape, v.dtype) for v in shapes]
        + [pltpu.SemaphoreType.DMA((n_in,)), pltpu.SemaphoreType.DMA((n_out + n_cut,))]
        + list(scratch),
        compiler_params=pltpu.CompilerParams(vmem_limit_bytes=mib * MIB),
        name=name,
    )(*args)


def on_device(
    hidden, gain, w_query, w_key, w_value, cotangent, seq_length, home_offset, dest_shard, dest_offset
):
    shards = NZ * NX * NC
    peers = lax.axis_size("tensor")
    me, z, x, c = place()
    strides = [-1, 1, shards // 2, shards // 2 + 1]
    width = hidden.shape[1]
    deep = width // 2
    q_cols = w_query.shape[1]
    k_cols = w_key.shape[1]
    q_heads = q_cols // HEAD
    rows_each = D // shards

    own = jnp.concatenate([w_query, w_key, w_value], 1)
    own_half = lax.all_to_all(
        jnp.broadcast_to(own[None], (NX,) + own.shape), "x", split_axis=0, concat_axis=0, tiled=True
    ).reshape(NX * own.shape[0], own.shape[1])
    own_half, cotangent = tied(own_half, cotangent)
    mine = lax.all_gather(own_half, "z", axis=0, tiled=True)

    half = HEAD // 2
    freq = np.power(np.float32(ROPE_BASE), -(np.arange(half, dtype=np.float32) * np.float32(2.0 / HEAD)))
    freq = jnp.asarray(np.concatenate([freq, freq])[None, :].astype(np.float32))
    square = ((TOK_DEV, TOK_DEV), F32)
    block = (2 * TOK_DEV + EXTRA, deep)
    cut = ((MAXLEN, q_cols), BF)
    wide = ((2 * MAXLEN, q_cols), BF)
    cot_near, cot_behind, cot_far, home, dest, cosine, sine, allowed, packed, order = kernel_call(
        functools.partial(plan_kernel, strides, shards),
        [wide, cut, cut] + [((SLOTS * MAXLEN, TOK_DEV), BF), ((SLOTS * MAXLEN, CAP), BF)] + [square] * 3
        + [(block, BF), ((width, width), BF)],
        [seq_length.T, home_offset.T, dest_shard.T, dest_offset.T, freq, cotangent, hidden, gain[None, :]],
        "plan", 60, 4,
    )
    copies = jnp.broadcast_to(packed[None], (peers,) + packed.shape)
    rows_full = lax.all_to_all(copies, "tensor", split_axis=0, concat_axis=0, tiled=True)
    cot_near = passed_along(cot_near, -1)
    cot_behind = passed_along(cot_behind, 1)
    cot_far = passed_along(jnp.concatenate([cot_far, cot_near[MAXLEN:]], 0), shards // 2)

    mine, rows_full, cot_near, cot_behind, cot_far = tied(
        mine, rows_full, cot_near, cot_behind, cot_far
    )
    theirs = other_core(mine)

    normed, inverse, partial, grad_out = kernel_call(
        norm_kernel,
        [((2, TOK_DEV, NZ * deep), BF), square, ((TOK_DEV, q_cols + 2 * k_cols), F32), ((q_heads * TOK_DEV, HEAD), BF)],
        [rows_full, mine, home, cot_near, cot_behind, cot_far], "norm", 60,
    )
    *attn_cuts, grad_value, terms = kernel_call(
        functools.partial(layer_kernel, q_heads),
        [cut] * 4 + [((TOK_DEV, k_cols), BF), ((peers,) + block, BF)],
        [normed, cosine, sine, allowed, home, grad_out, theirs, inverse, partial, mine],
        "layer", 60, 0,
        [pltpu.VMEM((TOK_DEV, q_cols + 2 * k_cols), BF)], 5, (6, 9),
    )
    total = lax.psum_scatter(terms, "tensor", scatter_dimension=0, tiled=False)
    (grad_hidden,) = kernel_call(
        finish_kernel, [((TOK_DEV, width), BF)],
        [packed, inverse, total, order], "finish", 60,
    )

    share = ((NZ * NX, rows_each, k_cols), BF)
    kept, given = kernel_call(value_kernel, [share, share], [normed, grad_value], "value", 12)
    pair = (kept.astype(F32) + other_core(given).astype(F32)).astype(BF)
    parts = lax.all_to_all(pair, ("z", "x"), split_axis=0, concat_axis=0, tiled=True)
    grad_value_weight = jnp.sum(parts.astype(F32), 0)

    attn_sent = [passed_along(attn_cuts[n], s) for n, s in enumerate(strides)]
    (attn_out,) = kernel_call(
        lay_kernel, [((CAP, q_cols), BF)], [dest, *attn_sent], "lay", 8
    )
    return (attn_out, grad_hidden, grad_value_weight)


def solution(mesh):
    fine = Mesh(mesh.devices.reshape(NZ, NX, NC, -1), DP + ("tensor",))
    both = P(DP, "tensor")
    return jax.shard_map(
        on_device,
        mesh=fine,
        in_specs=(both, P("tensor")) + (both,) * 4 + (P(),) * 4,
        out_specs=(both,) * 3,
        check_vma=False,
    )
```
